32 devices in a mesh: slab: 8 (over y, x, core), band: 4 (over z).
Axes of the slice: x: 2, y: 2, z: 4, core: 2. Of those that a mesh axis runs over, the one named last changes fastest.
Arguments:
- basis: float32 [3, 128, 12288], P(None, 'slab', 'band')
- offsets: float32 [3, 128, 64], P(None, 'slab', 'band'), may hold values from -0.45 to 0.45
- bond_modulus: float32 [128, 64], P('slab', 'band'), may hold values from 0.5 to 2
- bulk_modulus: float32 [128, 64], P('slab', 'band'), may hold values from 0.5 to 2
- springs: float32 [128, 64], P('slab', 'band'), may hold values from 0.5 to 2
- intact: int32 [8, 8, 9], P('slab', 'band'), may hold values from 0 to 1, as said below
Outputs:
- new_modes: float32 [3, 128, 4096], P(None, 'slab', 'band')
- new_images: float32 [3, 128, 4096], P(None, 'slab', 'band')
- reduced: float32 [64, 64], replicated
The draws below stay inside these ranges and needn't reach their ends.
Inputs may be any that keep to these rules, and one draw needn't show every extreme that they name: intact[i, j, 3 (dx + 1) + (dy + 1)] is 1 where the bonds between block (i, j) and block (i + dx, j + dy) are intact, and 0 where they are broken or that block lies outside the plate; the entry for (0, 0) is always 1, and the entry for (dx, dy) of one block equals the entry for (-dx, -dy) of the other.
All inputs are finite; a program needn't handle non-finite values.
Results may differ from the reference program's by a relative error of at most 0.0003.
Values sent between devices are 32-bit elements; how exact they have to be, the bound alone decides.
A program may use at most 128 MiB of HBM per device.

```python
import math
import jax
import jax.numpy as jnp
from jax import lax

BLOCK_X = 16
BLOCK_Y = 8
REACH = 3
MODES = 64
NCOL = 192
NX = 128
NY = 64
GX = 8
GY = 8


def draw_basis(key, part):
    noise_key, scale_key, column_key = jax.random.split(key, 3)
    full_shape = (3, NX, NY, NCOL)
    values = jax.random.normal(noise_key, full_shape, jnp.float32)
    point_scale = jnp.exp(jax.random.uniform(scale_key, (3, NX, NY, 1), jnp.float32, 0.0, math.log(10.0)))
    rising = jnp.exp(math.log(3.0) * jnp.arange(NX, dtype=jnp.float32) / NX).reshape(1, NX, 1, 1)
    column_scale = jnp.exp(jax.random.uniform(column_key, (NCOL,), jnp.float32, 0.0, math.log(10.0)))
    return (values * point_scale * rising * column_scale).reshape(3, NX, NY * NCOL)


def draw_intact(key, part):
    forward = (jax.random.randint(key, (4, GX, GY), 0, 4) > 0).astype(jnp.int32)
    along_x = jnp.arange(GX, dtype=jnp.int32)[:, None]
    along_y = jnp.arange(GY, dtype=jnp.int32)[None, :]
    directions = ((1, -1), (1, 0), (1, 1), (0, 1))
    entries = [jnp.ones((GX, GY), jnp.int32) for number in range(9)]
    for number in range(4):
        step_x, step_y = directions[number]
        inside = ((along_x + step_x >= 0) & (along_x + step_x < GX) & (along_y + step_y >= 0) & (along_y + step_y < GY)).astype(jnp.int32)
        bonded = forward[number] * inside
        padded = jnp.pad(bonded, 1)
        shifted = padded[1 - step_x:1 - step_x + GX, 1 - step_y:1 - step_y + GY]
        entries[3 * (step_x + 1) + step_y + 1] = bonded
        entries[3 * (1 - step_x) + 1 - step_y] = shifted
    return jnp.stack(entries, axis=-1)


def shard_levels(rng, dims, cuts, least, high):
    def one(axis_at, parts):
        heights = jax.random.uniform(jax.random.fold_in(jax.random.fold_in(rng, 6), axis_at), (parts,), jnp.float32, least / len(cuts), high / len(cuts))
        return jnp.repeat(jnp.exp(heights), dims[axis_at] // parts).reshape((-1,) + (1,) * (len(dims) - axis_at - 1))

    factor_of = one(*cuts[0])
    for cut in cuts[1:]:
        factor_of = factor_of * one(*cut)
    return factor_of


def setup_inputs(seed: int = 0) -> dict:
    streams_of = jax.random.split(jax.random.key(seed), 7)
    return {
        "basis": draw_basis(jax.random.fold_in(streams_of[6], 71), 0),
        "offsets": jnp.clip(jax.random.uniform(streams_of[1], (3, NX, NY), jnp.float32, -0.45, 0.45) * shard_levels(streams_of[1], (3, NX, NY), ((1, 8), (2, 4)), -0.4, 0.0), -0.45, 0.45),
        "bond_modulus": jnp.clip(jnp.exp(math.log(2.0) - 1.3862944 * jax.random.uniform(streams_of[2], (NX, NY), jnp.float32) ** shard_levels(streams_of[2], (NX, NY), ((0, 8), (1, 4)), -0.2, 0.2)), 0.5, 2.0),
        "bulk_modulus": jnp.clip(jnp.exp(math.log(2.0) - 1.3862944 * jax.random.uniform(streams_of[3], (NX, NY), jnp.float32) ** shard_levels(streams_of[3], (NX, NY), ((0, 8), (1, 4)), -0.2, 0.2)), 0.5, 2.0),
        "springs": jnp.clip(jnp.exp(math.log(2.0) - 1.3862944 * jax.random.uniform(streams_of[4], (NX, NY), jnp.float32) ** shard_levels(streams_of[4], (NX, NY), ((0, 8), (1, 4)), -0.2, 0.2)), 0.5, 2.0),
        "intact": draw_intact(jax.random.fold_in(streams_of[6], 71), 0),
    }


horizon_square = 9.0
bond_scale = 1.0 / 18.0
dilation_scale = 1.0 / 27.0
highest = lax.Precision.HIGHEST

def pair_geometry(home_offsets, home_x, home_y, far_offsets, far_x, far_y, intact_mask):
    bond_vector = jnp.stack([far_x[None, :] - home_x[:, None] + far_offsets[0][None, :] - home_offsets[0][:, None], far_y[None, :] - home_y[:, None] + far_offsets[1][None, :] - home_offsets[1][:, None], far_offsets[2][None, :] - home_offsets[2][:, None]], axis=1)
    distance = jnp.sum(bond_vector * bond_vector, axis=1)
    weight = jnp.maximum(1.0 - distance / horizon_square, 0.0) * intact_mask
    return (bond_vector, weight)

def stiffness_terms(bond_vector, weight, home_modulus, far_modulus, home_field, far_field):
    home_count = bond_vector.shape[0]
    far_count = bond_vector.shape[2]
    column_count = home_field.shape[2]
    weighted = weight[:, None, :] * bond_vector
    far_flat = far_field.reshape(3 * far_count, column_count)
    volume_change = jnp.dot(weighted.reshape(home_count, 3 * far_count), far_flat, precision=highest)
    volume_change = volume_change - jnp.einsum('nc,cnk->nk', jnp.sum(weighted, axis=2), home_field, precision=highest)
    coupling = weight * (home_modulus[:, None] + far_modulus[None, :]) * bond_scale
    leading = jnp.transpose(bond_vector, (1, 0, 2))
    tensor = coupling[None, :, None, :] * leading[:, :, None, :] * bond_vector[None, :, :, :]
    bond_force = jnp.einsum('cnd,dnk->cnk', jnp.sum(tensor, axis=3), home_field, precision=highest)
    bond_force = bond_force - jnp.dot(tensor.reshape(3 * home_count, 3 * far_count), far_flat, precision=highest).reshape(3, home_count, column_count)
    return (volume_change, bond_force)

def dilatation_terms(bond_vector, weight, home_value, far_value):
    home_count = bond_vector.shape[0]
    weighted = jnp.transpose(weight[:, None, :] * bond_vector, (1, 0, 2))
    remote = jnp.dot(weighted.reshape(3 * home_count, -1), far_value, precision=highest).reshape(3, home_count, far_value.shape[1])
    return -(remote + jnp.sum(weighted, axis=2)[:, :, None] * home_value[None, :, :])

def rotation(mass_gram, stiff_gram, mode_count):
    mass_factor = jnp.linalg.cholesky(mass_gram)
    left_solved = lax.linalg.triangular_solve(mass_factor, stiff_gram, left_side=True, lower=True)
    projected = lax.linalg.triangular_solve(mass_factor, left_solved.T, left_side=True, lower=True)
    projected = 0.5 * (projected + projected.T)
    stiff_factor = jnp.linalg.cholesky(projected)
    target = jnp.eye(stiff_gram.shape[0], mode_count, dtype=stiff_gram.dtype)
    forward = lax.linalg.triangular_solve(stiff_factor, target, left_side=True, lower=True)
    inverse = lax.linalg.triangular_solve(stiff_factor, forward, left_side=True, lower=True, transpose_a=True)
    normal = jnp.linalg.cholesky(jnp.dot(inverse.T, inverse, precision=highest))
    lifted = lax.linalg.triangular_solve(mass_factor, inverse, left_side=True, lower=True, transpose_a=True)
    return lax.linalg.triangular_solve(normal, lifted, left_side=False, lower=True, transpose_a=True)

def reference(basis, offsets, bond_modulus, bulk_modulus, springs, intact):
    basis = basis.reshape(3, NX, NY, NCOL)
    float_type = basis.dtype
    column_count = basis.shape[3]
    home_count = BLOCK_X * BLOCK_Y
    wide_x = BLOCK_X + 2 * REACH
    wide_y = BLOCK_Y + 2 * REACH
    zero_index = jnp.zeros((), jnp.int32)
    field_pad = jnp.pad(basis, ((0, 0), (REACH, REACH), (REACH, REACH), (0, 0)))
    offset_pad = jnp.pad(offsets, ((0, 0), (REACH, REACH), (REACH, REACH)))
    modulus_pad = jnp.pad(bond_modulus, ((REACH, REACH), (REACH, REACH)))
    home_ix = jnp.repeat(jnp.arange(BLOCK_X, dtype=jnp.int32), BLOCK_Y)
    home_iy = jnp.tile(jnp.arange(BLOCK_Y, dtype=jnp.int32), BLOCK_X)
    far_ix = jnp.repeat(jnp.arange(wide_x, dtype=jnp.int32) - REACH, wide_y)
    far_iy = jnp.tile(jnp.arange(wide_y, dtype=jnp.int32) - REACH, wide_x)
    far_code = 3 * (jnp.floor_divide(far_ix, BLOCK_X) + 1) + jnp.floor_divide(far_iy, BLOCK_Y) + 1
    home_x = home_ix.astype(float_type)
    home_y = home_iy.astype(float_type)
    far_x = far_ix.astype(float_type)
    far_y = far_iy.astype(float_type)
    block_ids = jnp.arange(GX * GY, dtype=jnp.int32)

    def geometry(block_id):
        block_row = (block_id // GY).astype(jnp.int32)
        block_col = (block_id % GY).astype(jnp.int32)
        start_x = block_row * BLOCK_X
        start_y = block_col * BLOCK_Y
        home_offsets = lax.dynamic_slice(offsets, (zero_index, start_x, start_y), (3, BLOCK_X, BLOCK_Y)).reshape(3, home_count)
        far_offsets = lax.dynamic_slice(offset_pad, (zero_index, start_x, start_y), (3, wide_x, wide_y)).reshape(3, wide_x * wide_y)
        bond_row = lax.dynamic_slice(intact, (block_row, block_col, zero_index), (1, 1, 9)).reshape(9).astype(float_type)
        intact_mask = jnp.zeros(far_code.shape, float_type)
        for offset in range(9):
            intact_mask = intact_mask + jnp.where(far_code == offset, bond_row[offset], 0.0)
        bond_vector, weight = pair_geometry(home_offsets, home_x, home_y, far_offsets, far_x, far_y, intact_mask[None, :])
        return (bond_vector, weight, start_x, start_y)

    def first_pass(block_id):
        bond_vector, weight, start_x, start_y = geometry(block_id)
        home_field = lax.dynamic_slice(basis, (zero_index, start_x, start_y, zero_index), (3, BLOCK_X, BLOCK_Y, column_count)).reshape(3, home_count, column_count)
        far_field = lax.dynamic_slice(field_pad, (zero_index, start_x, start_y, zero_index), (3, wide_x, wide_y, column_count)).reshape(3, wide_x * wide_y, column_count)
        home_modulus = lax.dynamic_slice(bond_modulus, (start_x, start_y), (BLOCK_X, BLOCK_Y)).reshape(home_count)
        far_modulus = lax.dynamic_slice(modulus_pad, (start_x, start_y), (wide_x, wide_y)).reshape(wide_x * wide_y)
        return stiffness_terms(bond_vector, weight, home_modulus, far_modulus, home_field, far_field)
    volumes, bond_blocks = lax.map(first_pass, block_ids)
    volume_grid = volumes.reshape(GX, GY, BLOCK_X, BLOCK_Y, column_count).transpose(0, 2, 1, 3, 4).reshape(NX, NY, column_count)
    bond_grid = bond_blocks.reshape(GX, GY, 3, BLOCK_X, BLOCK_Y, column_count).transpose(2, 0, 3, 1, 4, 5).reshape(3, NX, NY, column_count)
    dilatation = dilation_scale * bulk_modulus[:, :, None] * volume_grid
    dilatation_pad = jnp.pad(dilatation, ((REACH, REACH), (REACH, REACH), (0, 0)))

    def second_pass(block_id):
        bond_vector, weight, start_x, start_y = geometry(block_id)
        home_value = lax.dynamic_slice(dilatation, (start_x, start_y, zero_index), (BLOCK_X, BLOCK_Y, column_count)).reshape(home_count, column_count)
        far_value = lax.dynamic_slice(dilatation_pad, (start_x, start_y, zero_index), (wide_x, wide_y, column_count)).reshape(wide_x * wide_y, column_count)
        return dilatation_terms(bond_vector, weight, home_value, far_value)
    dilatation_blocks = lax.map(second_pass, block_ids)
    dilatation_grid = dilatation_blocks.reshape(GX, GY, 3, BLOCK_X, BLOCK_Y, column_count).transpose(2, 0, 3, 1, 4, 5).reshape(3, NX, NY, column_count)
    images = bond_grid + dilatation_grid + springs[None, :, :, None] * basis
    total_rows = 3.0 * NX * NY
    flat_basis = basis.reshape(-1, column_count)
    flat_images = images.reshape(-1, column_count)
    mass_gram = jnp.einsum('rk,rl->kl', flat_basis, flat_basis, precision=highest) / total_rows
    stiff_gram = jnp.einsum('rk,rl->kl', flat_basis, flat_images, precision=highest) / total_rows
    stiff_gram = 0.5 * (stiff_gram + stiff_gram.T)
    rotate = rotation(mass_gram, stiff_gram, MODES)
    new_modes = jnp.einsum('cxyk,km->cxym', basis, rotate, precision=highest)
    new_images = jnp.einsum('cxyk,km->cxym', images, rotate, precision=highest)
    reduced = jnp.einsum('cxym,cxyn->mn', new_modes, new_images, precision=highest) / total_rows
    return (new_modes.reshape(3, NX, NY * MODES), new_images.reshape(3, NX, NY * MODES), reduced)
```

```python
import functools

import jax
import jax.numpy as jnp
import numpy as np
from jax import lax
from jax.experimental import pallas as pl
from jax.experimental.pallas import tpu as pltpu
from jax.sharding import PartitionSpec as P

BLOCK_X = 16
BLOCK_Y = 8
REACH = 3
MODES = 64
NCOL = 192
WIDE = 256
MESH = pl.DeviceIdType.MESH
horizon_square = 9.0
bond_scale = 1.0 / 18.0
dilation_scale = 1.0 / 27.0


def dot(a, b, contract=((1,), (0,))):
    return lax.dot_general(
        a,
        b,
        (contract, ((), ())),
        precision=lax.Precision.HIGHEST,
        preferred_element_type=jnp.float32,
    )


def far_lattice(size_x, size_y):
    points = [(x, y) for x in range(size_x) for y in range(size_y)]
    low, high_x, high_y = range(-REACH, 0), range(size_x, size_x + REACH), range(size_y, size_y + REACH)
    points += [(x, y) for x in low for y in range(size_y)]
    points += [(x, y) for x in high_x for y in range(size_y)]
    points += [(x, y) for x in range(size_x) for y in low]
    points += [(x, y) for x in range(size_x) for y in high_y]
    for side_x in (low, high_x):
        for side_y in (low, high_y):
            points += [(x, y) for x in side_x for y in side_y] + [None] * (16 - REACH * REACH)
    return points


def constants(size_x, size_y):
    points = far_lattice(size_x, size_y)
    count = len(points)
    blocks = size_y // BLOCK_Y
    lattice = np.zeros((8, count), np.float32)
    chosen = np.zeros((blocks, 9, count), np.float32)
    for k, point in enumerate(points):
        if point is None:
            continue
        lattice[0, k], lattice[1, k] = point
        for b in range(blocks):
            dx, dy = point[0] // BLOCK_X, point[1] // BLOCK_Y - b
            if abs(dx) <= 1 and abs(dy) <= 1:
                chosen[b, 3 * (dx + 1) + dy + 1, k] = 1.0
    rows = [(x, y) for x in range(size_x) for y in range(REACH)]
    rows += [(x, y) for x in range(size_x) for y in range(size_y - REACH, size_y)]
    for side_x in (range(REACH), range(size_x - REACH, size_x)):
        for side_y in (range(REACH), range(size_y - REACH, size_y)):
            rows += [(x, y) for x in side_x for y in side_y] + [None] * (16 - REACH * REACH)
    pick = np.zeros((len(rows), size_x * size_y), np.float32)
    for r, point in enumerate(rows):
        if point is not None:
            pick[r, point[0] * size_y + point[1]] = 1.0
    return lattice, chosen, pick


def plate_kernel(
    shape,
    slabs,
    bands,
    reduce_here,
    total_rows,
    home_ref,
    mask_ref,
    lattice_ref,
    pick_ref,
    images_ref,
    gram_ref,
    far,
    edge,
    theta,
    theta_edge,
    tensor,
    lean,
    volume_lean,
    part,
    slots,
    mine,
    halo_send,
    halo_recv,
    theta_send,
    theta_recv,
    scatter_send,
    scatter_recv,
    gather_send,
    gather_recv,
):
    size_x, size_y = shape
    home = size_x * size_y
    edge_x, edge_y = REACH * size_y, REACH * size_x
    slab, band = lax.axis_index("slab"), lax.axis_index("band")
    devices = slabs * bands
    me = slab * bands + band
    left, right = lax.rem(slab + slabs - 1, slabs), lax.rem(slab + 1, slabs)
    down, up = lax.rem(band + bands - 1, bands), lax.rem(band + 1, bands)

    def peer(step):
        other = lax.rem(me + step, devices)
        return other, (lax.div(other, bands), lax.rem(other, bands))

    around = [
        (left, band), (right, band), (slab, down), (slab, up),
        (left, down), (left, up), (right, down), (right, up),
    ]
    barrier = pltpu.get_barrier_semaphore()
    if reduce_here:
        for step in range(1, devices):
            pl.semaphore_signal(barrier, inc=1, device_id=peer(step)[1], device_id_type=MESH)
    else:
        for target in around:
            pl.semaphore_signal(barrier, inc=1, device_id=target, device_id_type=MESH)

    at = [home, home + edge_x, home + 2 * edge_x, home + 2 * edge_x + edge_y]
    corner = home + 2 * edge_x + 2 * edge_y
    plan = [
        (True, 0, edge_x, at[1], around[0]),
        (True, home - edge_x, edge_x, at[0], around[1]),
        (False, 0, edge_y, at[3], around[2]),
        (False, edge_y, edge_y, at[2], around[3]),
        (False, 2 * edge_y, 16, corner + 48, around[4]),
        (False, 2 * edge_y + 16, 16, corner + 32, around[5]),
        (False, 2 * edge_y + 32, 16, corner + 16, around[6]),
        (False, 2 * edge_y + 48, 16, corner, around[7]),
    ]
    for c in range(3):
        edge[c] = dot(pick_ref[...], home_ref[c])
    pl.semaphore_wait(barrier, devices - 1 if reduce_here else 8)
    halo = []
    for number, (direct, start, rows, there, target) in enumerate(plan):
        source = home_ref if direct else edge
        copy = pltpu.make_async_remote_copy(
            src_ref=source.at[:, pl.ds(start, rows), :],
            dst_ref=far.at[:, pl.ds(there, rows), :],
            send_sem=halo_send.at[number],
            recv_sem=halo_recv.at[number],
            device_id=target,
            device_id_type=MESH,
        )
        copy.start()
        halo.append(copy)
    far[:, pl.ds(0, home), :] = home_ref[...]
    mass = jnp.zeros((WIDE, WIDE), jnp.float32)
    for c in range(3):
        mass = mass + dot(home_ref[c], home_ref[c], ((0,), (0,)))
    for copy in halo:
        copy.wait_recv()

    rows_far = jnp.transpose(far[0, :, 128:256])
    count = rows_far.shape[1]
    chunk = 64
    blocks = size_y // BLOCK_Y
    masks = jnp.broadcast_to(
        mask_ref[...].reshape(1, blocks, 1, count), (chunk // size_y, blocks, BLOCK_Y, count)
    ).reshape(chunk, count)
    lattice_x, lattice_y = lattice_ref[0:1, :], lattice_ref[1:2, :]
    for number in range(home // chunk):
        first = number * chunk
        side = home_ref[0, first : first + chunk, 128:256]
        point = lax.broadcasted_iota(jnp.int32, (chunk, 1), 0) + first
        home_x = (point // size_y).astype(jnp.float32)
        home_y = (point % size_y).astype(jnp.float32)
        bond = [
            (lattice_x - home_x) + (rows_far[64:65, :] - side[:, 64:65]),
            (lattice_y - home_y) + (rows_far[65:66, :] - side[:, 65:66]),
            rows_far[66:67, :] - side[:, 66:67],
        ]
        distance = bond[0] * bond[0] + bond[1] * bond[1] + bond[2] * bond[2]
        weight = jnp.maximum(1.0 - distance / horizon_square, 0.0) * masks
        coupling = weight * ((side[:, 67:68] + rows_far[67:68, :]) * bond_scale)
        itself = lax.broadcasted_iota(jnp.int32, (chunk, count), 1) == point
        springs = side[:, 69:70]
        for c in range(3):
            weighted = weight * bond[c]
            added = jnp.where(itself, jnp.sum(weighted, axis=1, keepdims=True), 0.0)
            lean[c * home + first : c * home + first + chunk, :] = weighted + added
            volume_lean[first : first + chunk, c * count : (c + 1) * count] = weighted - added
            leading = coupling * bond[c]
            for d in range(c, 3):
                entry = leading * bond[d]
                own = jnp.sum(entry, axis=1, keepdims=True)
                if c == d:
                    own = own + springs
                entry = jnp.where(itself, own, 0.0) - entry
                tensor[c * home + first : c * home + first + chunk, d * count : (d + 1) * count] = entry
                if c != d:
                    tensor[d * home + first : d * home + first + chunk, c * count : (c + 1) * count] = entry

    field = far[...].reshape(3 * count, WIDE)
    volume = dot(volume_lean[...], field)
    theta[pl.ds(0, home), :] = volume * (home_ref[0, :, 196:197] * dilation_scale)
    theta_edge[...] = dot(pick_ref[...], theta[pl.ds(0, home), :])
    moved = []
    for number, (direct, start, rows, there, target) in enumerate(plan):
        source = theta if direct else theta_edge
        copy = pltpu.make_async_remote_copy(
            src_ref=source.at[pl.ds(start, rows), :],
            dst_ref=theta.at[pl.ds(there, rows), :],
            send_sem=theta_send.at[number],
            recv_sem=theta_recv.at[number],
            device_id=target,
            device_id_type=MESH,
        )
        copy.start()
        moved.append(copy)
    force = dot(tensor[...], field)
    for copy in moved:
        copy.wait_recv()
    images = force - dot(lean[...], theta[...])
    images_ref[...] = images.reshape(3, home, WIDE)
    stiff = jnp.zeros((WIDE, WIDE), jnp.float32)
    for c in range(3):
        stiff = stiff + dot(home_ref[c], images[c * home : (c + 1) * home], ((0,), (0,)))
    stiff = 0.5 * (stiff + jnp.transpose(stiff))
    down_axis = lax.broadcasted_iota(jnp.int32, (WIDE, WIDE), 0)
    along = lax.broadcasted_iota(jnp.int32, (WIDE, WIDE), 1)
    own = jnp.sum(jnp.where(down_axis == along, stiff, 0.0), axis=1, keepdims=True)
    packed = jnp.where(along == NCOL, own, jnp.where(down_axis >= along, mass, stiff))
    packed = packed * (1.0 / total_rows)
    if not reduce_here:
        gram_ref[...] = packed
    else:
        part[...] = packed
        share = WIDE // devices
        copies = []
        for step in range(1, devices):
            other, target = peer(step)
            copy = pltpu.make_async_remote_copy(
                src_ref=part.at[pl.ds(pl.multiple_of(other * share, share), share), :],
                dst_ref=slots.at[step],
                send_sem=scatter_send.at[step],
                recv_sem=scatter_recv.at[step],
                device_id=target,
                device_id_type=MESH,
            )
            copy.start()
            copies.append(copy)
        here = pl.ds(pl.multiple_of(me * share, share), share)
        total = part[here, :]
        for step in range(1, devices):
            copies[step - 1].wait_recv()
            total = total + slots[step]
        mine[...] = total
        gathers = []
        for step in range(1, devices):
            copy = pltpu.make_async_remote_copy(
                src_ref=mine,
                dst_ref=gram_ref.at[here, :],
                send_sem=gather_send.at[step],
                recv_sem=gather_recv.at[step],
                device_id=peer(step)[1],
                device_id_type=MESH,
            )
            copy.start()
            gathers.append(copy)
        gram_ref[here, :] = total
        for copy in gathers:
            copy.wait_recv()
        for copy in copies + gathers:
            copy.wait_send()
    for copy in halo + moved:
        copy.wait_send()


def mode_kernel(gram_ref, home_ref, images_ref, modes_ref, new_images_ref, reduced_ref, table):
    packed = gram_ref[...]
    flipped = jnp.transpose(packed)
    down = lax.broadcasted_iota(jnp.int32, (WIDE, WIDE), 0)
    along = lax.broadcasted_iota(jnp.int32, (WIDE, WIDE), 1)
    diagonal = packed[:, NCOL : NCOL + 1]
    mass = jnp.where(down >= along, packed, flipped)
    stiff = jnp.where(down < along, packed, jnp.where(down == along, diagonal, flipped))
    mass = mass[:NCOL]
    stiff = stiff[:NCOL]
    column = along[:NCOL]
    table[...] = jnp.where(column < NCOL, stiff, pltpu.roll(mass, NCOL, 1))
    block = 32
    row_in = lax.broadcasted_iota(jnp.int32, (block, WIDE), 0)
    for start in range(0, NCOL, block):
        panel = table[start : start + block, :]
        for k in range(block):
            at = start + k
            row = panel[k : k + 1, :]
            scaled = row * (1.0 / row[:, at : at + 1])
            panel = jnp.where(row_in == k, scaled, panel - panel[:, at : at + 1] * scaled)
        whole = table[...]
        swept = whole - dot(whole[:, start : start + block], panel)
        table[...] = swept
        table[start : start + block, :] = panel
    solved = jnp.where(
        lax.broadcasted_iota(jnp.int32, (NCOL, 128), 1) < MODES,
        pltpu.roll(table[:, 128:256], 64, 1),
        0.0,
    )
    weighed = dot(mass[:, :NCOL], solved)
    normal = dot(solved, weighed, ((0,), (0,)))[:MODES]
    row_in = lax.broadcasted_iota(jnp.int32, (MODES, 128), 0)
    lane = lax.broadcasted_iota(jnp.int32, (MODES, 128), 1)
    normal = jnp.where(lane == row_in + MODES, 1.0, normal)
    for k in range(MODES):
        row = normal[k : k + 1, :]
        scaled = row * lax.rsqrt(row[:, k : k + 1])
        column = normal[:, k : k + 1] * lax.rsqrt(row[:, k : k + 1])
        normal = jnp.where(
            row_in == k, scaled, jnp.where(row_in > k, normal - column * scaled, normal)
        )
    rotate = dot(solved[:, :MODES], normal[:, MODES:], ((1,), (1,)))
    turned = dot(stiff[:, :NCOL], rotate)
    reduced_ref[...] = dot(rotate, turned, ((0,), (0,)))
    for c in range(3):
        modes_ref[c] = dot(home_ref[c][:, :NCOL], rotate)
        new_images_ref[c] = dot(images_ref[c][:, :NCOL], rotate)


def local(slabs, bands, basis, offsets, bond_modulus, bulk_modulus, springs, intact):
    size_x, size_y = offsets.shape[1:]
    home = size_x * size_y
    lattice, chosen, pick = constants(size_x, size_y)
    count = lattice.shape[1]
    devices = slabs * bands
    reduce_here = devices <= 32 and 32 % devices == 0
    total_rows = float(3 * home * devices)
    scalars = jnp.concatenate(
        [offsets.reshape(3, home), jnp.stack([bond_modulus, bulk_modulus, springs]).reshape(3, home)]
    ).T
    scalars = jnp.pad(scalars, ((0, 0), (0, WIDE - NCOL - 6)))[None]
    wide = jnp.concatenate(
        [basis.reshape(3, home, NCOL), jnp.pad(scalars, ((0, 2), (0, 0), (0, 0)))], axis=2
    )
    mask = jnp.sum(intact[0].astype(jnp.float32)[:, :, None] * chosen, axis=1)
    vmem = pl.BlockSpec(memory_space=pltpu.VMEM)
    f32 = jnp.float32
    images, gram = pl.pallas_call(
        functools.partial(
            plate_kernel, (size_x, size_y), slabs, bands, reduce_here, total_rows
        ),
        out_shape=(
            jax.ShapeDtypeStruct((3, home, WIDE), f32),
            jax.ShapeDtypeStruct((WIDE, WIDE), f32),
        ),
        in_specs=[vmem] * 4,
        out_specs=(vmem, vmem),
        scratch_shapes=[
            pltpu.VMEM((3, count, WIDE), f32),
            pltpu.VMEM((3, pick.shape[0], WIDE), f32),
            pltpu.VMEM((count, WIDE), f32),
            pltpu.VMEM((pick.shape[0], WIDE), f32),
            pltpu.VMEM((3 * home, 3 * count), f32),
            pltpu.VMEM((3 * home, count), f32),
            pltpu.VMEM((home, 3 * count), f32),
            pltpu.VMEM((WIDE, WIDE), f32),
            pltpu.VMEM((devices, max(WIDE // devices, 8), WIDE), f32),
            pltpu.VMEM((max(WIDE // devices, 8), WIDE), f32),
        ]
        + [pltpu.SemaphoreType.DMA((8,))] * 4
        + [pltpu.SemaphoreType.DMA((devices,))] * 4,
        compiler_params=pltpu.CompilerParams(
            collective_id=0, has_side_effects=True, vmem_limit_bytes=48 << 20
        ),
    )(wide, mask, lattice, pick)
    if not reduce_here:
        gram = lax.psum(gram, ("slab", "band"))
    modes, new_images, reduced = pl.pallas_call(
        mode_kernel,
        out_shape=(
            jax.ShapeDtypeStruct((3, home, MODES), f32),
            jax.ShapeDtypeStruct((3, home, MODES), f32),
            jax.ShapeDtypeStruct((MODES, MODES), f32),
        ),
        in_specs=[vmem] * 3,
        out_specs=(vmem,) * 3,
        scratch_shapes=[pltpu.VMEM((NCOL, WIDE), f32)],
        compiler_params=pltpu.CompilerParams(vmem_limit_bytes=48 << 20),
    )(gram, wide, images)
    return (
        modes.reshape(3, size_x, size_y * MODES),
        new_images.reshape(3, size_x, size_y * MODES),
        reduced,
    )


def solution(mesh):
    in_specs = (
        P(None, "slab", "band"),
        P(None, "slab", "band"),
        P("slab", "band"),
        P("slab", "band"),
        P("slab", "band"),
        P("slab", "band", None),
    )
    out_specs = (P(None, "slab", "band"), P(None, "slab", "band"), P())
    body = functools.partial(local, mesh.shape["slab"], mesh.shape["band"])
    return jax.shard_map(body, mesh=mesh, in_specs=in_specs, out_specs=out_specs, check_vma=False)
```

```python
import functools

import jax
import jax.numpy as jnp
import numpy as np
from jax import lax
from jax.experimental import pallas as pl
from jax.experimental.pallas import tpu as pltpu
from jax.sharding import PartitionSpec as P

BLOCK_X = 16
BLOCK_Y = 8
REACH = 3
MODES = 64
NCOL = 192
WIDE = 256
MESH = pl.DeviceIdType.MESH
horizon_square = 9.0
bond_scale = 1.0 / 18.0
dilation_scale = 1.0 / 27.0


def dot(a, b, contract=((1,), (0,))):
    return lax.dot_general(
        a,
        b,
        (contract, ((), ())),
        precision=lax.Precision.HIGHEST,
        preferred_element_type=jnp.float32,
    )


def split(value):
    high = value.astype(jnp.bfloat16)
    return high, (value - high.astype(jnp.float32)).astype(jnp.bfloat16)


def narrow_dot(a, b, contract=((1,), (0,))):
    return lax.dot_general(
        a, b, (contract, ((), ())), preferred_element_type=jnp.float32
    )


def split_dot(a, b, contract=((1,), (0,))):
    small = narrow_dot(a[0], b[1], contract) + narrow_dot(a[1], b[0], contract)
    return small + narrow_dot(a[0], b[0], contract)


def picked(pick, value):
    first, rest = split(value)
    second = value - first.astype(jnp.float32)
    third = (second - rest.astype(jnp.float32)).astype(jnp.bfloat16)
    return narrow_dot(pick, first) + (narrow_dot(pick, rest) + narrow_dot(pick, third))


def far_lattice(size_x, size_y):
    points = [(x, y) for x in range(size_x) for y in range(size_y)]
    low, high_x, high_y = range(-REACH, 0), range(size_x, size_x + REACH), range(size_y, size_y + REACH)
    points += [(x, y) for x in low for y in range(size_y)]
    points += [(x, y) for x in high_x for y in range(size_y)]
    points += [(x, y) for x in range(size_x) for y in low]
    points += [(x, y) for x in range(size_x) for y in high_y]
    for side_x in (low, high_x):
        for side_y in (low, high_y):
            points += [(x, y) for x in side_x for y in side_y] + [None] * (16 - REACH * REACH)
    return points


def constants(size_x, size_y):
    points = far_lattice(size_x, size_y)
    count = len(points)
    blocks = size_y // BLOCK_Y
    lattice = np.zeros((8, count), np.float32)
    chosen = np.zeros((blocks, 9, count), np.float32)
    for k, point in enumerate(points):
        if point is None:
            continue
        lattice[0, k], lattice[1, k] = point
        for b in range(blocks):
            dx, dy = point[0] // BLOCK_X, point[1] // BLOCK_Y - b
            if abs(dx) <= 1 and abs(dy) <= 1:
                chosen[b, 3 * (dx + 1) + dy + 1, k] = 1.0
    rows = [(x, y) for x in range(size_x) for y in range(REACH)]
    rows += [(x, y) for x in range(size_x) for y in range(size_y - REACH, size_y)]
    for side_x in (range(REACH), range(size_x - REACH, size_x)):
        for side_y in (range(REACH), range(size_y - REACH, size_y)):
            rows += [(x, y) for x in side_x for y in side_y] + [None] * (16 - REACH * REACH)
    pick = np.zeros((len(rows), size_x * size_y), np.float32)
    for r, point in enumerate(rows):
        if point is not None:
            pick[r, point[0] * size_y + point[1]] = 1.0
    return lattice, chosen, pick.astype(jnp.bfloat16)


def plate_kernel(
    shape,
    slabs,
    bands,
    reduce_here,
    total_rows,
    home_ref,
    mask_ref,
    lattice_ref,
    pick_ref,
    images_ref,
    gram_ref,
    far,
    edge,
    theta,
    theta_edge,
    tensor,
    tensor_low,
    lean,
    lean_low,
    volume_lean,
    volume_lean_low,
    field,
    field_low,
    part,
    slots,
    mine,
    halo_send,
    halo_recv,
    theta_send,
    theta_recv,
    scatter_send,
    scatter_recv,
    gather_send,
    gather_recv,
):
    size_x, size_y = shape
    home = size_x * size_y
    edge_x, edge_y = REACH * size_y, REACH * size_x
    slab, band = lax.axis_index("slab"), lax.axis_index("band")
    devices = slabs * bands
    me = slab * bands + band
    left, right = lax.rem(slab + slabs - 1, slabs), lax.rem(slab + 1, slabs)
    down, up = lax.rem(band + bands - 1, bands), lax.rem(band + 1, bands)

    def peer(step):
        other = lax.rem(me + step, devices)
        return other, (lax.div(other, bands), lax.rem(other, bands))

    around = [
        (left, band), (right, band), (slab, down), (slab, up),
        (left, down), (left, up), (right, down), (right, up),
    ]
    barrier = pltpu.get_barrier_semaphore()
    if reduce_here:
        for step in range(1, devices):
            pl.semaphore_signal(barrier, inc=1, device_id=peer(step)[1], device_id_type=MESH)
    else:
        for target in around:
            pl.semaphore_signal(barrier, inc=1, device_id=target, device_id_type=MESH)

    at = [home, home + edge_x, home + 2 * edge_x, home + 2 * edge_x + edge_y]
    corner = home + 2 * edge_x + 2 * edge_y
    has_left, has_right = slab > 0, slab < slabs - 1
    has_down, has_up = band > 0, band < bands - 1
    exists = [
        has_left, has_right, has_down, has_up,
        has_left & has_down, has_left & has_up, has_right & has_down, has_right & has_up,
    ]
    opposite = [1, 0, 3, 2, 7, 6, 5, 4]
    plan = [
        (True, 0, edge_x, at[1], around[0]),
        (True, home - edge_x, edge_x, at[0], around[1]),
        (False, 0, edge_y, at[3], around[2]),
        (False, edge_y, edge_y, at[2], around[3]),
        (False, 2 * edge_y, 16, corner + 48, around[4]),
        (False, 2 * edge_y + 16, 16, corner + 32, around[5]),
        (False, 2 * edge_y + 32, 16, corner + 16, around[6]),
        (False, 2 * edge_y + 48, 16, corner, around[7]),
    ]
    for c in range(3):
        edge[c] = picked(pick_ref[...], home_ref[c])
    pl.semaphore_wait(barrier, devices - 1 if reduce_here else 8)
    halo = []
    for number, (direct, start, rows, there, target) in enumerate(plan):
        source = home_ref if direct else edge
        copy = pltpu.make_async_remote_copy(
            src_ref=source.at[:, pl.ds(start, rows), :],
            dst_ref=far.at[:, pl.ds(there, rows), :],
            send_sem=halo_send.at[number],
            recv_sem=halo_recv.at[number],
            device_id=target,
            device_id_type=MESH,
        )
        pl.when(exists[number])(copy.start)
        halo.append(copy)

        @pl.when(jnp.logical_not(exists[opposite[number]]))
        def clear(there=there, rows=rows):
            far[:, pl.ds(there, rows), :] = jnp.zeros((3, rows, WIDE), jnp.float32)
            theta[pl.ds(there, rows), :] = jnp.zeros((rows, WIDE), jnp.float32)
    far[:, pl.ds(0, home), :] = home_ref[...]
    home_parts = split(home_ref[...].reshape(3 * home, WIDE))
    mass = split_dot(home_parts, home_parts, ((0,), (0,)))
    for number, copy in enumerate(halo):
        pl.when(exists[opposite[number]])(copy.wait_recv)

    rows_far = jnp.transpose(far[0, :, 128:256])
    count = rows_far.shape[1]
    chunk = 64
    blocks = size_y // BLOCK_Y
    masks = jnp.broadcast_to(
        mask_ref[...].reshape(1, blocks, 1, count), (chunk // size_y, blocks, BLOCK_Y, count)
    ).reshape(chunk, count)
    lattice_x, lattice_y = lattice_ref[0:1, :], lattice_ref[1:2, :]

    @pl.loop(0, home // chunk)
    def build(number):
        first = pl.multiple_of(number * chunk, chunk)
        side = home_ref[0, pl.ds(first, chunk), 128:256]
        point = lax.broadcasted_iota(jnp.int32, (chunk, 1), 0) + first
        home_x = (point // size_y).astype(jnp.float32)
        home_y = (point % size_y).astype(jnp.float32)
        bond = [
            (lattice_x - home_x) + (rows_far[64:65, :] - side[:, 64:65]),
            (lattice_y - home_y) + (rows_far[65:66, :] - side[:, 65:66]),
            rows_far[66:67, :] - side[:, 66:67],
        ]
        distance = bond[0] * bond[0] + bond[1] * bond[1] + bond[2] * bond[2]
        weight = jnp.maximum(1.0 - distance / horizon_square, 0.0) * masks
        coupling = weight * ((side[:, 67:68] + rows_far[67:68, :]) * bond_scale)
        itself = lax.broadcasted_iota(jnp.int32, (chunk, count), 1) == point
        springs = side[:, 69:70]
        for c in range(3):
            weighted = weight * bond[c]
            added = jnp.where(itself, jnp.sum(weighted, axis=1, keepdims=True), 0.0)
            rows = pl.ds(c * home + first, chunk)
            lean[rows, :], lean_low[rows, :] = split(weighted + added)
            here = (pl.ds(first, chunk), slice(c * count, (c + 1) * count))
            volume_lean[here], volume_lean_low[here] = split(weighted - added)
            leading = coupling * bond[c]
            for d in range(c, 3):
                entry = leading * bond[d]
                own = jnp.sum(entry, axis=1, keepdims=True)
                if c == d:
                    own = own + springs
                high, low = split(jnp.where(itself, own, 0.0) - entry)
                here = (rows, slice(d * count, (d + 1) * count))
                tensor[here], tensor_low[here] = high, low
                if c != d:
                    here = (pl.ds(d * home + first, chunk), slice(c * count, (c + 1) * count))
                    tensor[here], tensor_low[here] = high, low

    field[...], field_low[...] = split(far[...].reshape(3 * count, WIDE))
    field_parts = (field[...], field_low[...])
    volume = split_dot((volume_lean[...], volume_lean_low[...]), field_parts)
    theta[pl.ds(0, home), :] = volume * (home_ref[0, :, 196:197] * dilation_scale)
    theta_edge[...] = picked(pick_ref[...], theta[pl.ds(0, home), :])
    moved = []
    for number, (direct, start, rows, there, target) in enumerate(plan):
        source = theta if direct else theta_edge
        copy = pltpu.make_async_remote_copy(
            src_ref=source.at[pl.ds(start, rows), :],
            dst_ref=theta.at[pl.ds(there, rows), :],
            send_sem=theta_send.at[number],
            recv_sem=theta_recv.at[number],
            device_id=target,
            device_id_type=MESH,
        )
        pl.when(exists[number])(copy.start)
        moved.append(copy)

    @pl.loop(0, 3)
    def forces(c):
        rows = pl.ds(pl.multiple_of(c * home, home), home)
        images_ref[c] = split_dot((tensor[rows, :], tensor_low[rows, :]), (field[...], field_low[...]))

    for number, copy in enumerate(moved):
        pl.when(exists[opposite[number]])(copy.wait_recv)
    theta_parts = split(theta[...])
    images = images_ref[...].reshape(3 * home, WIDE) - split_dot(
        (lean[...], lean_low[...]), theta_parts
    )
    images_ref[...] = images.reshape(3, home, WIDE)
    stiff = split_dot(home_parts, split(images), ((0,), (0,)))
    stiff = 0.5 * (stiff + jnp.transpose(stiff))
    down_axis = lax.broadcasted_iota(jnp.int32, (WIDE, WIDE), 0)
    along = lax.broadcasted_iota(jnp.int32, (WIDE, WIDE), 1)
    own = jnp.sum(jnp.where(down_axis == along, stiff, 0.0), axis=1, keepdims=True)
    packed = jnp.where(along == NCOL, own, jnp.where(down_axis >= along, mass, stiff))
    packed = packed * (1.0 / total_rows)
    if not reduce_here:
        gram_ref[...] = packed
    else:
        part[...] = packed
        share = WIDE // devices
        copies = []
        for step in range(1, devices):
            other, target = peer(step)
            copy = pltpu.make_async_remote_copy(
                src_ref=part.at[pl.ds(pl.multiple_of(other * share, share), share), :],
                dst_ref=slots.at[step],
                send_sem=scatter_send.at[step],
                recv_sem=scatter_recv.at[step],
                device_id=target,
                device_id_type=MESH,
            )
            copy.start()
            copies.append(copy)
        here = pl.ds(pl.multiple_of(me * share, share), share)
        total = part[here, :]
        for step in range(1, devices):
            copies[step - 1].wait_recv()
            total = total + slots[step]
        mine[...] = total
        gathers = []
        for step in range(1, devices):
            copy = pltpu.make_async_remote_copy(
                src_ref=mine,
                dst_ref=gram_ref.at[here, :],
                send_sem=gather_send.at[step],
                recv_sem=gather_recv.at[step],
                device_id=peer(step)[1],
                device_id_type=MESH,
            )
            copy.start()
            gathers.append(copy)
        gram_ref[here, :] = total
        for copy in gathers:
            copy.wait_recv()
        for copy in copies + gathers:
            copy.wait_send()
    for number in range(8):
        pl.when(exists[number])(halo[number].wait_send)
        pl.when(exists[number])(moved[number].wait_send)


def mode_kernel(gram_ref, home_ref, images_ref, modes_ref, new_images_ref, reduced_ref, table):
    packed = gram_ref[...]
    flipped = jnp.transpose(packed)
    down = lax.broadcasted_iota(jnp.int32, (WIDE, WIDE), 0)
    along = lax.broadcasted_iota(jnp.int32, (WIDE, WIDE), 1)
    diagonal = packed[:, NCOL : NCOL + 1]
    mass = jnp.where(down >= along, packed, flipped)
    stiff = jnp.where(down < along, packed, jnp.where(down == along, diagonal, flipped))
    mass = mass[:NCOL]
    stiff = stiff[:NCOL]
    column = along[:NCOL]
    level = lax.rsqrt(diagonal[:NCOL])
    level_row = lax.rsqrt(
        jnp.sum(jnp.where(down[:NCOL] == column, stiff, 0.0), axis=0, keepdims=True)
    )
    table[...] = level * jnp.where(column < NCOL, stiff * level_row, pltpu.roll(mass, NCOL, 1))
    block = 64
    row_in = lax.broadcasted_iota(jnp.int32, (block, WIDE), 0)
    for start in range(0, NCOL, block):
        panel = table[start : start + block, :]
        for k in range(0, block, 2):
            at = start + k
            row, next_row = panel[k : k + 1, :], panel[k + 1 : k + 2, :]
            a, b = row[:, at : at + 1], row[:, at + 1 : at + 2]
            c, d = next_row[:, at : at + 1], next_row[:, at + 1 : at + 2]
            inverse = 1.0 / (a * d - b * c)
            one = (d * row - b * next_row) * inverse
            two = (a * next_row - c * row) * inverse
            swept = panel - panel[:, at : at + 1] * one - panel[:, at + 1 : at + 2] * two
            panel = jnp.where(row_in == k, one, jnp.where(row_in == k + 1, two, swept))
        whole = table[...]
        table[...] = whole - dot(whole[:, start : start + block], panel)
        table[start : start + block, :] = panel
    solved = jnp.where(
        lax.broadcasted_iota(jnp.int32, (NCOL, 128), 1) < MODES,
        level * pltpu.roll(table[:, 128:256], 64, 1),
        0.0,
    )
    weighed = dot(mass[:, :NCOL], solved)
    normal = dot(solved, weighed, ((0,), (0,)))[:MODES]
    row_in = lax.broadcasted_iota(jnp.int32, (MODES, 128), 0)
    lane = lax.broadcasted_iota(jnp.int32, (MODES, 128), 1)
    corner = jnp.where(lane == row_in, normal, 0.0)
    level = lax.rsqrt(jnp.sum(corner, axis=1, keepdims=True))
    level_row = lax.rsqrt(jnp.sum(corner, axis=0, keepdims=True))
    normal = jnp.where(
        lane < MODES,
        level * normal * level_row,
        jnp.where(lane == row_in + MODES, level, 0.0),
    )
    for k in range(0, MODES, 2):
        row, next_row = normal[k : k + 1, :], normal[k + 1 : k + 2, :]
        a, b = row[:, k : k + 1], row[:, k + 1 : k + 2]
        c, d = next_row[:, k : k + 1], next_row[:, k + 1 : k + 2]
        first = lax.rsqrt(a)
        second = first * lax.rsqrt(a * d - b * c)
        one = row * first
        two = (a * next_row - c * row) * second
        left, right = normal[:, k : k + 1], normal[:, k + 1 : k + 2]
        swept = normal - (left * first) * one - ((a * right - b * left) * second) * two
        normal = jnp.where(
            row_in == k,
            one,
            jnp.where(row_in == k + 1, two, jnp.where(row_in > k, swept, normal)),
        )
    rotate = dot(solved[:, :MODES], normal[:, MODES:], ((1,), (1,)))
    turned = dot(stiff[:, :NCOL], rotate)
    reduced_ref[...] = dot(rotate, turned, ((0,), (0,)))
    rotate_parts = split(rotate)
    for source, target in ((home_ref, modes_ref), (images_ref, new_images_ref)):
        for c in range(3):
            target[c] = split_dot(split(source[c][:, :NCOL]), rotate_parts)


def local(slabs, bands, basis, offsets, bond_modulus, bulk_modulus, springs, intact):
    size_x, size_y = offsets.shape[1:]
    home = size_x * size_y
    lattice, chosen, pick = constants(size_x, size_y)
    count = lattice.shape[1]
    devices = slabs * bands
    reduce_here = devices <= 32 and 32 % devices == 0
    total_rows = float(3 * home * devices)
    scalars = jnp.concatenate(
        [offsets.reshape(3, home), jnp.stack([bond_modulus, bulk_modulus, springs]).reshape(3, home)]
    ).T
    scalars = jnp.pad(scalars, ((0, 0), (0, WIDE - NCOL - 6)))[None]
    wide = jnp.concatenate(
        [basis.reshape(3, home, NCOL), jnp.pad(scalars, ((0, 2), (0, 0), (0, 0)))], axis=2
    )
    mask = jnp.sum(intact[0].astype(jnp.float32)[:, :, None] * chosen, axis=1)
    vmem = pl.BlockSpec(memory_space=pltpu.VMEM)
    f32 = jnp.float32
    images, gram = pl.pallas_call(
        functools.partial(
            plate_kernel, (size_x, size_y), slabs, bands, reduce_here, total_rows
        ),
        out_shape=(
            jax.ShapeDtypeStruct((3, home, WIDE), f32),
            jax.ShapeDtypeStruct((WIDE, WIDE), f32),
        ),
        in_specs=[vmem] * 4,
        out_specs=(vmem, vmem),
        scratch_shapes=[
            pltpu.VMEM((3, count, WIDE), f32),
            pltpu.VMEM((3, pick.shape[0], WIDE), f32),
            pltpu.VMEM((count, WIDE), f32),
            pltpu.VMEM((pick.shape[0], WIDE), f32),
            pltpu.VMEM((3 * home, 3 * count), jnp.bfloat16),
            pltpu.VMEM((3 * home, 3 * count), jnp.bfloat16),
            pltpu.VMEM((3 * home, count), jnp.bfloat16),
            pltpu.VMEM((3 * home, count), jnp.bfloat16),
            pltpu.VMEM((home, 3 * count), jnp.bfloat16),
            pltpu.VMEM((home, 3 * count), jnp.bfloat16),
            pltpu.VMEM((3 * count, WIDE), jnp.bfloat16),
            pltpu.VMEM((3 * count, WIDE), jnp.bfloat16),
            pltpu.VMEM((WIDE, WIDE), f32),
            pltpu.VMEM((devices, max(WIDE // devices, 8), WIDE), f32),
            pltpu.VMEM((max(WIDE // devices, 8), WIDE), f32),
        ]
        + [pltpu.SemaphoreType.DMA((8,))] * 4
        + [pltpu.SemaphoreType.DMA((devices,))] * 4,
        compiler_params=pltpu.CompilerParams(
            collective_id=0, has_side_effects=True, vmem_limit_bytes=48 << 20
        ),
    )(wide, mask, lattice, pick)
    if not reduce_here:
        gram = lax.psum(gram, ("slab", "band"))
    modes, new_images, reduced = pl.pallas_call(
        mode_kernel,
        out_shape=(
            jax.ShapeDtypeStruct((3, home, MODES), f32),
            jax.ShapeDtypeStruct((3, home, MODES), f32),
            jax.ShapeDtypeStruct((MODES, MODES), f32),
        ),
        in_specs=[vmem] * 3,
        out_specs=(vmem,) * 3,
        scratch_shapes=[pltpu.VMEM((NCOL, WIDE), f32)],
        compiler_params=pltpu.CompilerParams(vmem_limit_bytes=48 << 20),
    )(gram, wide, images)
    return (
        modes.reshape(3, size_x, size_y * MODES),
        new_images.reshape(3, size_x, size_y * MODES),
        reduced,
    )


def solution(mesh):
    in_specs = (
        P(None, "slab", "band"),
        P(None, "slab", "band"),
        P("slab", "band"),
        P("slab", "band"),
        P("slab", "band"),
        P("slab", "band", None),
    )
    out_specs = (P(None, "slab", "band"), P(None, "slab", "band"), P())
    body = functools.partial(local, mesh.shape["slab"], mesh.shape["band"])
    return jax.shard_map(body, mesh=mesh, in_specs=in_specs, out_specs=out_specs, check_vma=False)
```

```python
import functools

import jax
import jax.numpy as jnp
import numpy as np
from jax import lax
from jax.experimental import pallas as pl
from jax.experimental.pallas import tpu as pltpu
from jax.sharding import PartitionSpec as P

BLOCK_X = 16
BLOCK_Y = 8
REACH = 3
MODES = 64
NCOL = 192
WIDE = 256
MESH = pl.DeviceIdType.MESH
horizon_square = 9.0
bond_scale = 1.0 / 18.0
dilation_scale = 1.0 / 27.0


def dot(a, b, contract=((1,), (0,))):
    return lax.dot_general(
        a,
        b,
        (contract, ((), ())),
        precision=lax.Precision.HIGHEST,
        preferred_element_type=jnp.float32,
    )


def split(value):
    high = value.astype(jnp.bfloat16)
    return high, (value - high.astype(jnp.float32)).astype(jnp.bfloat16)


def narrow_dot(a, b, contract=((1,), (0,))):
    return lax.dot_general(
        a, b, (contract, ((), ())), preferred_element_type=jnp.float32
    )


def split_dot(a, b, contract=((1,), (0,))):
    small = narrow_dot(a[0], b[1], contract) + narrow_dot(a[1], b[0], contract)
    return small + narrow_dot(a[0], b[0], contract)


def picked(pick, value):
    first, rest = split(value)
    second = value - first.astype(jnp.float32)
    third = (second - rest.astype(jnp.float32)).astype(jnp.bfloat16)
    return narrow_dot(pick, first) + (narrow_dot(pick, rest) + narrow_dot(pick, third))


def far_lattice(size_x, size_y):
    points = [(x, y) for x in range(size_x) for y in range(size_y)]
    low, high_x, high_y = range(-REACH, 0), range(size_x, size_x + REACH), range(size_y, size_y + REACH)
    points += [(x, y) for x in low for y in range(size_y)]
    points += [(x, y) for x in high_x for y in range(size_y)]
    points += [(x, y) for x in range(size_x) for y in low]
    points += [(x, y) for x in range(size_x) for y in high_y]
    for side_x in (low, high_x):
        for side_y in (low, high_y):
            points += [(x, y) for x in side_x for y in side_y] + [None] * (16 - REACH * REACH)
    return points


def constants(size_x, size_y):
    points = far_lattice(size_x, size_y)
    count = len(points)
    blocks = size_y // BLOCK_Y
    lattice = np.zeros((8, count), np.float32)
    chosen = np.zeros((blocks, 9, count), np.float32)
    for k, point in enumerate(points):
        if point is None:
            continue
        lattice[0, k], lattice[1, k] = point
        for b in range(blocks):
            dx, dy = point[0] // BLOCK_X, point[1] // BLOCK_Y - b
            if abs(dx) <= 1 and abs(dy) <= 1:
                chosen[b, 3 * (dx + 1) + dy + 1, k] = 1.0
    rows = [(x, y) for x in range(size_x) for y in range(REACH)]
    rows += [(x, y) for x in range(size_x) for y in range(size_y - REACH, size_y)]
    for side_x in (range(REACH), range(size_x - REACH, size_x)):
        for side_y in (range(REACH), range(size_y - REACH, size_y)):
            rows += [(x, y) for x in side_x for y in side_y] + [None] * (16 - REACH * REACH)
    pick = np.zeros((len(rows), size_x * size_y), np.float32)
    for r, point in enumerate(rows):
        if point is not None:
            pick[r, point[0] * size_y + point[1]] = 1.0
    return lattice, chosen, pick.astype(jnp.bfloat16)


def plate_kernel(
    shape,
    slabs,
    bands,
    reduce_here,
    total_rows,
    home_ref,
    mask_ref,
    lattice_ref,
    pick_ref,
    images_ref,
    gram_ref,
    far,
    edge,
    theta,
    theta_edge,
    tensor,
    tensor_low,
    lean,
    lean_low,
    volume_lean,
    volume_lean_low,
    field,
    field_low,
    part,
    slots,
    mine,
    halo_send,
    halo_recv,
    theta_send,
    theta_recv,
    scatter_send,
    scatter_recv,
    gather_send,
    gather_recv,
):
    size_x, size_y = shape
    home = size_x * size_y
    edge_x, edge_y = REACH * size_y, REACH * size_x
    slab, band = lax.axis_index("slab"), lax.axis_index("band")
    devices = slabs * bands
    me = slab * bands + band
    left, right = lax.rem(slab + slabs - 1, slabs), lax.rem(slab + 1, slabs)
    down, up = lax.rem(band + bands - 1, bands), lax.rem(band + 1, bands)

    def peer(step):
        other = lax.rem(me + step, devices)
        return other, (lax.div(other, bands), lax.rem(other, bands))

    around = [
        (left, band), (right, band), (slab, down), (slab, up),
        (left, down), (left, up), (right, down), (right, up),
    ]
    barrier = pltpu.get_barrier_semaphore()
    if reduce_here:
        for step in range(1, devices):
            pl.semaphore_signal(barrier, inc=1, device_id=peer(step)[1], device_id_type=MESH)
    else:
        for target in around:
            pl.semaphore_signal(barrier, inc=1, device_id=target, device_id_type=MESH)

    at = [home, home + edge_x, home + 2 * edge_x, home + 2 * edge_x + edge_y]
    corner = home + 2 * edge_x + 2 * edge_y
    has_left, has_right = slab > 0, slab < slabs - 1
    has_down, has_up = band > 0, band < bands - 1
    exists = [
        has_left, has_right, has_down, has_up,
        has_left & has_down, has_left & has_up, has_right & has_down, has_right & has_up,
    ]
    opposite = [1, 0, 3, 2, 7, 6, 5, 4]
    plan = [
        (True, 0, edge_x, at[1], around[0]),
        (True, home - edge_x, edge_x, at[0], around[1]),
        (False, 0, edge_y, at[3], around[2]),
        (False, edge_y, edge_y, at[2], around[3]),
        (False, 2 * edge_y, 16, corner + 48, around[4]),
        (False, 2 * edge_y + 16, 16, corner + 32, around[5]),
        (False, 2 * edge_y + 32, 16, corner + 16, around[6]),
        (False, 2 * edge_y + 48, 16, corner, around[7]),
    ]
    for c in range(3):
        edge[c] = picked(pick_ref[...], home_ref[c])
    pl.semaphore_wait(barrier, devices - 1 if reduce_here else 8)
    pieces = [
        (pl.ds(0, 1), pl.ds(128, 128)),
        (pl.ds(0, 1), pl.ds(0, 128)),
        (pl.ds(1, 2), pl.ds(0, WIDE)),
    ]
    halo = []
    for number, (direct, start, rows, there, target) in enumerate(plan):
        source = home_ref if direct else edge
        copies = []
        for piece, (parts, lanes) in enumerate(pieces):
            copy = pltpu.make_async_remote_copy(
                src_ref=source.at[parts, pl.ds(start, rows), lanes],
                dst_ref=far.at[parts, pl.ds(there, rows), lanes],
                send_sem=halo_send.at[3 * number + piece],
                recv_sem=halo_recv.at[3 * number + piece],
                device_id=target,
                device_id_type=MESH,
            )
            copies.append(copy)
        pl.when(exists[number])(copies[0].start)
        halo.append(copies)

        @pl.when(jnp.logical_not(exists[opposite[number]]))
        def clear(there=there, rows=rows):
            far[:, pl.ds(there, rows), :] = jnp.zeros((3, rows, WIDE), jnp.float32)
            theta[pl.ds(there, rows), :] = jnp.zeros((rows, WIDE), jnp.float32)
    for number, copies in enumerate(halo):
        for copy in copies[1:]:
            pl.when(exists[number])(copy.start)
    far[:, pl.ds(0, home), :] = home_ref[...]
    home_parts = split(home_ref[...].reshape(3 * home, WIDE))
    mass = split_dot(home_parts, home_parts, ((0,), (0,)))
    for number, copies in enumerate(halo):
        pl.when(exists[opposite[number]])(copies[0].wait_recv)

    rows_far = jnp.transpose(far[0, :, 128:256])
    count = rows_far.shape[1]
    chunk = 64
    blocks = size_y // BLOCK_Y
    masks = jnp.broadcast_to(
        mask_ref[...].reshape(1, blocks, 1, count), (chunk // size_y, blocks, BLOCK_Y, count)
    ).reshape(chunk, count)
    lattice_x, lattice_y = lattice_ref[0:1, :], lattice_ref[1:2, :]

    @pl.loop(0, home // chunk)
    def build(number):
        first = pl.multiple_of(number * chunk, chunk)
        side = home_ref[0, pl.ds(first, chunk), 128:256]
        point = lax.broadcasted_iota(jnp.int32, (chunk, 1), 0) + first
        home_x = (point // size_y).astype(jnp.float32)
        home_y = (point % size_y).astype(jnp.float32)
        bond = [
            (lattice_x - home_x) + (rows_far[64:65, :] - side[:, 64:65]),
            (lattice_y - home_y) + (rows_far[65:66, :] - side[:, 65:66]),
            rows_far[66:67, :] - side[:, 66:67],
        ]
        distance = bond[0] * bond[0] + bond[1] * bond[1] + bond[2] * bond[2]
        weight = jnp.maximum(1.0 - distance / horizon_square, 0.0) * masks
        coupling = weight * ((side[:, 67:68] + rows_far[67:68, :]) * bond_scale)
        itself = lax.broadcasted_iota(jnp.int32, (chunk, count), 1) == point
        springs = side[:, 69:70]
        for c in range(3):
            weighted = weight * bond[c]
            added = jnp.where(itself, jnp.sum(weighted, axis=1, keepdims=True), 0.0)
            rows = pl.ds(c * home + first, chunk)
            lean[rows, :], lean_low[rows, :] = split(weighted + added)
            here = (pl.ds(first, chunk), slice(c * count, (c + 1) * count))
            volume_lean[here], volume_lean_low[here] = split(weighted - added)
            leading = coupling * bond[c]
            for d in range(c, 3):
                entry = leading * bond[d]
                own = jnp.sum(entry, axis=1, keepdims=True)
                if c == d:
                    own = own + springs
                high, low = split(jnp.where(itself, own, 0.0) - entry)
                here = (rows, slice(d * count, (d + 1) * count))
                tensor[here], tensor_low[here] = high, low
                if c != d:
                    here = (pl.ds(d * home + first, chunk), slice(c * count, (c + 1) * count))
                    tensor[here], tensor_low[here] = high, low

    for number, copies in enumerate(halo):
        for copy in copies[1:]:
            pl.when(exists[opposite[number]])(copy.wait_recv)
    field[...], field_low[...] = split(far[...].reshape(3 * count, WIDE))
    field_parts = (field[...], field_low[...])
    volume = split_dot((volume_lean[...], volume_lean_low[...]), field_parts)
    theta[pl.ds(0, home), :] = volume * (home_ref[0, :, 196:197] * dilation_scale)
    theta_edge[...] = picked(pick_ref[...], theta[pl.ds(0, home), :])
    moved = []
    for number, (direct, start, rows, there, target) in enumerate(plan):
        source = theta if direct else theta_edge
        copy = pltpu.make_async_remote_copy(
            src_ref=source.at[pl.ds(start, rows), :],
            dst_ref=theta.at[pl.ds(there, rows), :],
            send_sem=theta_send.at[number],
            recv_sem=theta_recv.at[number],
            device_id=target,
            device_id_type=MESH,
        )
        pl.when(exists[number])(copy.start)
        moved.append(copy)

    @pl.loop(0, 3)
    def forces(c):
        rows = pl.ds(pl.multiple_of(c * home, home), home)
        images_ref[c] = split_dot((tensor[rows, :], tensor_low[rows, :]), (field[...], field_low[...]))

    for number, copy in enumerate(moved):
        pl.when(exists[opposite[number]])(copy.wait_recv)
    theta_parts = split(theta[...])
    images = images_ref[...].reshape(3 * home, WIDE) - split_dot(
        (lean[...], lean_low[...]), theta_parts
    )
    images_ref[...] = images.reshape(3, home, WIDE)
    stiff = split_dot(home_parts, split(images), ((0,), (0,)))
    stiff = 0.5 * (stiff + jnp.transpose(stiff))
    down_axis = lax.broadcasted_iota(jnp.int32, (WIDE, WIDE), 0)
    along = lax.broadcasted_iota(jnp.int32, (WIDE, WIDE), 1)
    own = jnp.sum(jnp.where(down_axis == along, stiff, 0.0), axis=1, keepdims=True)
    packed = jnp.where(along == NCOL, own, jnp.where(down_axis >= along, mass, stiff))
    packed = packed * (1.0 / total_rows)
    if not reduce_here:
        gram_ref[...] = packed
    else:
        part[...] = packed
        share = WIDE // devices
        copies = []
        for step in range(1, devices):
            other, target = peer(step)
            copy = pltpu.make_async_remote_copy(
                src_ref=part.at[pl.ds(pl.multiple_of(other * share, share), share), :],
                dst_ref=slots.at[step],
                send_sem=scatter_send.at[step],
                recv_sem=scatter_recv.at[step],
                device_id=target,
                device_id_type=MESH,
            )
            copy.start()
            copies.append(copy)
        here = pl.ds(pl.multiple_of(me * share, share), share)
        total = part[here, :]
        for step in range(1, devices):
            copies[step - 1].wait_recv()
            total = total + slots[step]
        mine[...] = total
        gathers = []
        for step in range(1, devices):
            copy = pltpu.make_async_remote_copy(
                src_ref=mine,
                dst_ref=gram_ref.at[here, :],
                send_sem=gather_send.at[step],
                recv_sem=gather_recv.at[step],
                device_id=peer(step)[1],
                device_id_type=MESH,
            )
            copy.start()
            gathers.append(copy)
        gram_ref[here, :] = total
        for copy in gathers:
            copy.wait_recv()
        for copy in copies + gathers:
            copy.wait_send()
    for number in range(8):
        for copy in halo[number]:
            pl.when(exists[number])(copy.wait_send)
        pl.when(exists[number])(moved[number].wait_send)


def mode_kernel(gram_ref, home_ref, images_ref, modes_ref, new_images_ref, reduced_ref, table):
    packed = gram_ref[...]
    flipped = jnp.transpose(packed)
    down = lax.broadcasted_iota(jnp.int32, (WIDE, WIDE), 0)
    along = lax.broadcasted_iota(jnp.int32, (WIDE, WIDE), 1)
    diagonal = packed[:, NCOL : NCOL + 1]
    mass = jnp.where(down >= along, packed, flipped)
    stiff = jnp.where(down < along, packed, jnp.where(down == along, diagonal, flipped))
    mass = mass[:NCOL]
    stiff = stiff[:NCOL]
    column = along[:NCOL]
    level = lax.rsqrt(diagonal[:NCOL])
    level_row = lax.rsqrt(
        jnp.sum(jnp.where(down[:NCOL] == column, stiff, 0.0), axis=0, keepdims=True)
    )
    table[...] = level * jnp.where(column < NCOL, stiff * level_row, pltpu.roll(mass, NCOL, 1))
    block = 64
    row_in = lax.broadcasted_iota(jnp.int32, (8, 128), 0)
    full = (8, 128)
    for start in range(0, NCOL, block):
        used = range(start // 128, 2)
        panel = {
            (g, h): table[start + 8 * g : start + 8 * g + 8, 128 * h : 128 * h + 128]
            for g in range(block // 8)
            for h in used
        }
        for k in range(0, block, 2):
            side, lane = divmod(start + k, 128)
            group, place = divmod(k, 8)
            left = [jnp.broadcast_to(panel[g, side][:, lane : lane + 1], full) for g in range(block // 8)]
            right = [
                jnp.broadcast_to(panel[g, side][:, lane + 1 : lane + 2], full) for g in range(block // 8)
            ]
            a, b = left[group][place : place + 1], right[group][place : place + 1]
            c, d = left[group][place + 1 : place + 2], right[group][place + 1 : place + 2]
            inverse = 1.0 / (a * d - b * c)
            a, b, c, d = a * inverse, b * inverse, c * inverse, d * inverse
            for h in used:
                row, next_row = panel[group, h][place : place + 1], panel[group, h][place + 1 : place + 2]
                one = jnp.broadcast_to(d * row - b * next_row, full)
                two = jnp.broadcast_to(a * next_row - c * row, full)
                for g in range(block // 8):
                    swept = panel[g, h] - left[g] * one - right[g] * two
                    if g == group:
                        swept = jnp.where(
                            row_in == place, one, jnp.where(row_in == place + 1, two, swept)
                        )
                    panel[g, h] = swept
        whole = [jnp.concatenate([panel[g, h] for g in range(block // 8)], axis=0) for h in used]
        columns = table[:, start : start + block]
        for h in used:
            lanes = slice(128 * h, 128 * h + 128)
            table[:, lanes] = table[:, lanes] - dot(columns, whole[h - used[0]])
            table[start : start + block, lanes] = whole[h - used[0]]
    solved = jnp.where(
        lax.broadcasted_iota(jnp.int32, (NCOL, 128), 1) < MODES,
        level * pltpu.roll(table[:, 128:256], 64, 1),
        0.0,
    )
    weighed = dot(mass[:, :NCOL], solved)
    normal = dot(solved, weighed, ((0,), (0,)))[:MODES]
    row_in = lax.broadcasted_iota(jnp.int32, (MODES, 128), 0)
    lane = lax.broadcasted_iota(jnp.int32, (MODES, 128), 1)
    corner = jnp.where(lane == row_in, normal, 0.0)
    level = lax.rsqrt(jnp.sum(corner, axis=1, keepdims=True))
    level_row = lax.rsqrt(jnp.sum(corner, axis=0, keepdims=True))
    normal = jnp.where(
        lane < MODES,
        level * normal * level_row,
        jnp.where(lane == row_in + MODES, level, 0.0),
    )
    panel = [normal[8 * g : 8 * g + 8] for g in range(MODES // 8)]
    row_in = lax.broadcasted_iota(jnp.int32, (8, 128), 0)
    for k in range(0, MODES, 2):
        group, place = divmod(k, 8)
        rest = range(group, MODES // 8)
        left = {g: jnp.broadcast_to(panel[g][:, k : k + 1], full) for g in rest}
        right = {g: jnp.broadcast_to(panel[g][:, k + 1 : k + 2], full) for g in rest}
        a, b = left[group][place : place + 1], right[group][place : place + 1]
        c, d = left[group][place + 1 : place + 2], right[group][place + 1 : place + 2]
        first = lax.rsqrt(a)
        second = first * lax.rsqrt(a * d - b * c)
        row, next_row = panel[group][place : place + 1], panel[group][place + 1 : place + 2]
        one = row * first
        two = (a * next_row - c * row) * second
        one_over, two_over = one * first, two * second
        for g in rest:
            swept = panel[g] - left[g] * one_over - (a * right[g] - b * left[g]) * two_over
            if g == group:
                swept = jnp.where(row_in > place, swept, panel[g])
                swept = jnp.where(row_in == place, one, jnp.where(row_in == place + 1, two, swept))
            panel[g] = swept
    normal = jnp.concatenate(panel, axis=0)
    rotate = dot(solved[:, :MODES], normal[:, MODES:], ((1,), (1,)))
    turned = dot(stiff[:, :NCOL], rotate)
    reduced_ref[...] = dot(rotate, turned, ((0,), (0,)))
    rotate_parts = split(rotate)
    for source, target in ((home_ref, modes_ref), (images_ref, new_images_ref)):
        for c in range(3):
            target[c] = split_dot(split(source[c][:, :NCOL]), rotate_parts)


def local(slabs, bands, basis, offsets, bond_modulus, bulk_modulus, springs, intact):
    size_x, size_y = offsets.shape[1:]
    home = size_x * size_y
    lattice, chosen, pick = constants(size_x, size_y)
    count = lattice.shape[1]
    devices = slabs * bands
    reduce_here = devices <= 32 and 32 % devices == 0
    total_rows = float(3 * home * devices)
    scalars = jnp.concatenate(
        [offsets, bond_modulus[None], bulk_modulus[None], springs[None]]
    ).reshape(6, home).T
    scalars = jnp.pad(scalars, ((0, 0), (0, WIDE - NCOL - 6)))[None]
    wide = jnp.concatenate(
        [basis.reshape(3, home, NCOL), jnp.pad(scalars, ((0, 2), (0, 0), (0, 0)))], axis=2
    )
    mask = jnp.sum(intact[0].astype(jnp.float32)[:, :, None] * chosen, axis=1)
    vmem = pl.BlockSpec(memory_space=pltpu.VMEM)
    f32 = jnp.float32
    images, gram = pl.pallas_call(
        functools.partial(
            plate_kernel, (size_x, size_y), slabs, bands, reduce_here, total_rows
        ),
        out_shape=(
            jax.ShapeDtypeStruct((3, home, WIDE), f32),
            jax.ShapeDtypeStruct((WIDE, WIDE), f32),
        ),
        in_specs=[vmem] * 4,
        out_specs=(vmem, vmem),
        scratch_shapes=[
            pltpu.VMEM((3, count, WIDE), f32),
            pltpu.VMEM((3, pick.shape[0], WIDE), f32),
            pltpu.VMEM((count, WIDE), f32),
            pltpu.VMEM((pick.shape[0], WIDE), f32),
            pltpu.VMEM((3 * home, 3 * count), jnp.bfloat16),
            pltpu.VMEM((3 * home, 3 * count), jnp.bfloat16),
            pltpu.VMEM((3 * home, count), jnp.bfloat16),
            pltpu.VMEM((3 * home, count), jnp.bfloat16),
            pltpu.VMEM((home, 3 * count), jnp.bfloat16),
            pltpu.VMEM((home, 3 * count), jnp.bfloat16),
            pltpu.VMEM((3 * count, WIDE), jnp.bfloat16),
            pltpu.VMEM((3 * count, WIDE), jnp.bfloat16),
            pltpu.VMEM((WIDE, WIDE), f32),
            pltpu.VMEM((devices, max(WIDE // devices, 8), WIDE), f32),
            pltpu.VMEM((max(WIDE // devices, 8), WIDE), f32),
        ]
        + [pltpu.SemaphoreType.DMA((24,))] * 4
        + [pltpu.SemaphoreType.DMA((devices,))] * 4,
        compiler_params=pltpu.CompilerParams(
            collective_id=0, has_side_effects=True, vmem_limit_bytes=48 << 20
        ),
    )(wide, mask, lattice, pick)
    if not reduce_here:
        gram = lax.psum(gram, ("slab", "band"))
    modes, new_images, reduced = pl.pallas_call(
        mode_kernel,
        out_shape=(
            jax.ShapeDtypeStruct((3, home, MODES), f32),
            jax.ShapeDtypeStruct((3, home, MODES), f32),
            jax.ShapeDtypeStruct((MODES, MODES), f32),
        ),
        in_specs=[vmem] * 3,
        out_specs=(vmem,) * 3,
        scratch_shapes=[pltpu.VMEM((NCOL, WIDE), f32)],
        compiler_params=pltpu.CompilerParams(vmem_limit_bytes=48 << 20),
    )(gram, wide, images)
    return (
        modes.reshape(3, size_x, size_y * MODES),
        new_images.reshape(3, size_x, size_y * MODES),
        reduced,
    )


def solution(mesh):
    in_specs = (
        P(None, "slab", "band"),
        P(None, "slab", "band"),
        P("slab", "band"),
        P("slab", "band"),
        P("slab", "band"),
        P("slab", "band", None),
    )
    out_specs = (P(None, "slab", "band"), P(None, "slab", "band"), P())
    body = functools.partial(local, mesh.shape["slab"], mesh.shape["band"])
    return jax.shard_map(body, mesh=mesh, in_specs=in_specs, out_specs=out_specs, check_vma=False)
```

```python
import functools

import jax
import jax.numpy as jnp
import numpy as np
from jax import lax
from jax.experimental import pallas as pl
from jax.experimental.pallas import tpu as pltpu
from jax.sharding import PartitionSpec as P

BLOCK_X = 16
BLOCK_Y = 8
REACH = 3
MODES = 64
NCOL = 192
WIDE = 256
MESH = pl.DeviceIdType.MESH
horizon_square = 9.0
bond_scale = 1.0 / 18.0
dilation_scale = 1.0 / 27.0


def dot(a, b, contract=((1,), (0,))):
    return lax.dot_general(
        a,
        b,
        (contract, ((), ())),
        precision=lax.Precision.HIGHEST,
        preferred_element_type=jnp.float32,
    )


def split(value):
    high = value.astype(jnp.bfloat16)
    return high, (value - high.astype(jnp.float32)).astype(jnp.bfloat16)


def narrow_dot(a, b, contract=((1,), (0,))):
    return lax.dot_general(
        a, b, (contract, ((), ())), preferred_element_type=jnp.float32
    )


def split_dot(a, b, contract=((1,), (0,))):
    small = narrow_dot(a[0], b[1], contract) + narrow_dot(a[1], b[0], contract)
    return small + narrow_dot(a[0], b[0], contract)


def picked(pick, value):
    first, rest = split(value)
    second = value - first.astype(jnp.float32)
    third = (second - rest.astype(jnp.float32)).astype(jnp.bfloat16)
    return narrow_dot(pick, first) + (narrow_dot(pick, rest) + narrow_dot(pick, third))


def far_lattice(size_x, size_y):
    points = [(x, y) for x in range(size_x) for y in range(size_y)]
    low, high_x, high_y = range(-REACH, 0), range(size_x, size_x + REACH), range(size_y, size_y + REACH)
    points += [(x, y) for x in low for y in range(size_y)]
    points += [(x, y) for x in high_x for y in range(size_y)]
    points += [(x, y) for x in range(size_x) for y in low]
    points += [(x, y) for x in range(size_x) for y in high_y]
    for side_x in (low, high_x):
        for side_y in (low, high_y):
            points += [(x, y) for x in side_x for y in side_y] + [None] * (16 - REACH * REACH)
    return points


def constants(size_x, size_y):
    points = far_lattice(size_x, size_y)
    count = len(points)
    blocks = size_y // BLOCK_Y
    lattice = np.zeros((8, count), np.float32)
    chosen = np.zeros((blocks, 9, count), np.float32)
    for k, point in enumerate(points):
        if point is None:
            continue
        lattice[0, k], lattice[1, k] = point
        for b in range(blocks):
            dx, dy = point[0] // BLOCK_X, point[1] // BLOCK_Y - b
            if abs(dx) <= 1 and abs(dy) <= 1:
                chosen[b, 3 * (dx + 1) + dy + 1, k] = 1.0
    rows = [(x, y) for x in range(size_x) for y in range(REACH)]
    rows += [(x, y) for x in range(size_x) for y in range(size_y - REACH, size_y)]
    for side_x in (range(REACH), range(size_x - REACH, size_x)):
        for side_y in (range(REACH), range(size_y - REACH, size_y)):
            rows += [(x, y) for x in side_x for y in side_y] + [None] * (16 - REACH * REACH)
    pick = np.zeros((len(rows), size_x * size_y), np.float32)
    for r, point in enumerate(rows):
        if point is not None:
            pick[r, point[0] * size_y + point[1]] = 1.0
    return lattice, chosen, pick.astype(jnp.bfloat16)


def plate_kernel(
    shape,
    slabs,
    bands,
    reduce_here,
    total_rows,
    home_ref,
    mask_ref,
    lattice_ref,
    pick_ref,
    images_ref,
    gram_ref,
    far,
    edge,
    theta,
    theta_edge,
    tensor,
    tensor_low,
    lean,
    lean_low,
    volume_lean,
    volume_lean_low,
    field,
    field_low,
    part,
    slots,
    mine,
    halo_send,
    halo_recv,
    theta_send,
    theta_recv,
    scatter_send,
    scatter_recv,
    gather_send,
    gather_recv,
):
    size_x, size_y = shape
    home = size_x * size_y
    edge_x, edge_y = REACH * size_y, REACH * size_x
    slab, band = lax.axis_index("slab"), lax.axis_index("band")
    devices = slabs * bands
    me = slab * bands + band
    left, right = lax.rem(slab + slabs - 1, slabs), lax.rem(slab + 1, slabs)
    down, up = lax.rem(band + bands - 1, bands), lax.rem(band + 1, bands)

    def peer(step):
        other = lax.rem(me + step, devices)
        return other, (lax.div(other, bands), lax.rem(other, bands))

    around = [
        (left, band), (right, band), (slab, down), (slab, up),
        (left, down), (left, up), (right, down), (right, up),
    ]
    barrier = pltpu.get_barrier_semaphore()
    if reduce_here:
        for step in range(1, devices):
            pl.semaphore_signal(barrier, inc=1, device_id=peer(step)[1], device_id_type=MESH)
    else:
        for target in around:
            pl.semaphore_signal(barrier, inc=1, device_id=target, device_id_type=MESH)

    at = [home, home + edge_x, home + 2 * edge_x, home + 2 * edge_x + edge_y]
    corner = home + 2 * edge_x + 2 * edge_y
    has_left, has_right = slab > 0, slab < slabs - 1
    has_down, has_up = band > 0, band < bands - 1
    exists = [
        has_left, has_right, has_down, has_up,
        has_left & has_down, has_left & has_up, has_right & has_down, has_right & has_up,
    ]
    opposite = [1, 0, 3, 2, 7, 6, 5, 4]
    plan = [
        (True, 0, edge_x, at[1], around[0]),
        (True, home - edge_x, edge_x, at[0], around[1]),
        (False, 0, edge_y, at[3], around[2]),
        (False, edge_y, edge_y, at[2], around[3]),
        (False, 2 * edge_y, 16, corner + 48, around[4]),
        (False, 2 * edge_y + 16, 16, corner + 32, around[5]),
        (False, 2 * edge_y + 32, 16, corner + 16, around[6]),
        (False, 2 * edge_y + 48, 16, corner, around[7]),
    ]
    for c in range(3):
        edge[c] = picked(pick_ref[...], home_ref[c])
    pl.semaphore_wait(barrier, devices - 1 if reduce_here else 8)
    pieces = [
        (pl.ds(0, 1), pl.ds(128, 128)),
        (pl.ds(0, 1), pl.ds(0, 128)),
        (pl.ds(1, 2), pl.ds(0, WIDE)),
    ]
    halo = []
    for number, (direct, start, rows, there, target) in enumerate(plan):
        source = home_ref if direct else edge
        copies = []
        for piece, (parts, lanes) in enumerate(pieces):
            copy = pltpu.make_async_remote_copy(
                src_ref=source.at[parts, pl.ds(start, rows), lanes],
                dst_ref=far.at[parts, pl.ds(there, rows), lanes],
                send_sem=halo_send.at[3 * number + piece],
                recv_sem=halo_recv.at[3 * number + piece],
                device_id=target,
                device_id_type=MESH,
            )
            copies.append(copy)
        pl.when(exists[number])(copies[0].start)
        halo.append(copies)

        @pl.when(jnp.logical_not(exists[opposite[number]]))
        def clear(there=there, rows=rows):
            far[:, pl.ds(there, rows), :] = jnp.zeros((3, rows, WIDE), jnp.float32)
            theta[pl.ds(there, rows), :] = jnp.zeros((rows, WIDE), jnp.float32)
    for number, copies in enumerate(halo):
        for copy in copies[1:]:
            pl.when(exists[number])(copy.start)
    far[:, pl.ds(0, home), :] = home_ref[...]
    home_parts = split(home_ref[...].reshape(3 * home, WIDE))
    mass = split_dot(home_parts, home_parts, ((0,), (0,)))
    for number, copies in enumerate(halo):
        pl.when(exists[opposite[number]])(copies[0].wait_recv)

    rows_far = jnp.transpose(far[0, :, 128:256])
    count = rows_far.shape[1]
    chunk = 64
    blocks = size_y // BLOCK_Y
    masks = jnp.broadcast_to(
        mask_ref[...].reshape(1, blocks, 1, count), (chunk // size_y, blocks, BLOCK_Y, count)
    ).reshape(chunk, count)
    lattice_x, lattice_y = lattice_ref[0:1, :], lattice_ref[1:2, :]

    @pl.loop(0, home // chunk)
    def build(number):
        first = pl.multiple_of(number * chunk, chunk)
        side = home_ref[0, pl.ds(first, chunk), 128:256]
        point = lax.broadcasted_iota(jnp.int32, (chunk, 1), 0) + first
        home_x = (point // size_y).astype(jnp.float32)
        home_y = (point % size_y).astype(jnp.float32)
        bond = [
            (lattice_x - home_x) + (rows_far[64:65, :] - side[:, 64:65]),
            (lattice_y - home_y) + (rows_far[65:66, :] - side[:, 65:66]),
            rows_far[66:67, :] - side[:, 66:67],
        ]
        distance = bond[0] * bond[0] + bond[1] * bond[1] + bond[2] * bond[2]
        weight = jnp.maximum(1.0 - distance / horizon_square, 0.0) * masks
        coupling = weight * ((side[:, 67:68] + rows_far[67:68, :]) * bond_scale)
        itself = lax.broadcasted_iota(jnp.int32, (chunk, count), 1) == point
        springs = side[:, 69:70]
        for c in range(3):
            weighted = weight * bond[c]
            added = jnp.where(itself, jnp.sum(weighted, axis=1, keepdims=True), 0.0)
            rows = pl.ds(c * home + first, chunk)
            lean[rows, :], lean_low[rows, :] = split(weighted + added)
            here = (pl.ds(first, chunk), slice(c * count, (c + 1) * count))
            volume_lean[here], volume_lean_low[here] = split(weighted - added)
            leading = coupling * bond[c]
            for d in range(c, 3):
                entry = leading * bond[d]
                own = jnp.sum(entry, axis=1, keepdims=True)
                if c == d:
                    own = own + springs
                high, low = split(jnp.where(itself, own, 0.0) - entry)
                here = (rows, slice(d * count, (d + 1) * count))
                tensor[here], tensor_low[here] = high, low
                if c != d:
                    here = (pl.ds(d * home + first, chunk), slice(c * count, (c + 1) * count))
                    tensor[here], tensor_low[here] = high, low

    for number, copies in enumerate(halo):
        for copy in copies[1:]:
            pl.when(exists[opposite[number]])(copy.wait_recv)
    field[...], field_low[...] = split(far[...].reshape(3 * count, WIDE))
    field_parts = (field[...], field_low[...])
    volume = split_dot((volume_lean[...], volume_lean_low[...]), field_parts)
    theta[pl.ds(0, home), :] = volume * (home_ref[0, :, 196:197] * dilation_scale)
    theta_edge[...] = picked(pick_ref[...], theta[pl.ds(0, home), :])
    moved = []
    for number, (direct, start, rows, there, target) in enumerate(plan):
        source = theta if direct else theta_edge
        copy = pltpu.make_async_remote_copy(
            src_ref=source.at[pl.ds(start, rows), :],
            dst_ref=theta.at[pl.ds(there, rows), :],
            send_sem=theta_send.at[number],
            recv_sem=theta_recv.at[number],
            device_id=target,
            device_id_type=MESH,
        )
        pl.when(exists[number])(copy.start)
        moved.append(copy)

    @pl.loop(0, 3)
    def forces(c):
        rows = pl.ds(pl.multiple_of(c * home, home), home)
        images_ref[c] = split_dot((tensor[rows, :], tensor_low[rows, :]), (field[...], field_low[...]))

    for number, copy in enumerate(moved):
        pl.when(exists[opposite[number]])(copy.wait_recv)
    theta_parts = split(theta[...])
    images = images_ref[...].reshape(3 * home, WIDE) - split_dot(
        (lean[...], lean_low[...]), theta_parts
    )
    images_ref[...] = images.reshape(3, home, WIDE)
    stiff = split_dot(home_parts, split(images), ((0,), (0,)))
    stiff = 0.5 * (stiff + jnp.transpose(stiff))
    down_axis = lax.broadcasted_iota(jnp.int32, (WIDE, WIDE), 0)
    along = lax.broadcasted_iota(jnp.int32, (WIDE, WIDE), 1)
    own = jnp.sum(jnp.where(down_axis == along, stiff, 0.0), axis=1, keepdims=True)
    packed = jnp.where(along == NCOL, own, jnp.where(down_axis >= along, mass, stiff))
    packed = packed * (1.0 / total_rows)
    if not reduce_here:
        gram_ref[...] = packed
    else:
        part[...] = packed
        share = WIDE // devices
        copies = []
        for step in range(1, devices):
            other, target = peer(step)
            copy = pltpu.make_async_remote_copy(
                src_ref=part.at[pl.ds(pl.multiple_of(other * share, share), share), :],
                dst_ref=slots.at[step],
                send_sem=scatter_send.at[step],
                recv_sem=scatter_recv.at[step],
                device_id=target,
                device_id_type=MESH,
            )
            copy.start()
            copies.append(copy)
        here = pl.ds(pl.multiple_of(me * share, share), share)
        total = part[here, :]
        for step in range(1, devices):
            copies[step - 1].wait_recv()
            total = total + slots[step]
        mine[...] = total
        gathers = []
        for step in range(1, devices):
            copy = pltpu.make_async_remote_copy(
                src_ref=mine,
                dst_ref=gram_ref.at[here, :],
                send_sem=gather_send.at[step],
                recv_sem=gather_recv.at[step],
                device_id=peer(step)[1],
                device_id_type=MESH,
            )
            copy.start()
            gathers.append(copy)
        gram_ref[here, :] = total
        for copy in gathers:
            copy.wait_recv()
        for copy in copies + gathers:
            copy.wait_send()
    for number in range(8):
        for copy in halo[number]:
            pl.when(exists[number])(copy.wait_send)
        pl.when(exists[number])(moved[number].wait_send)


def mode_kernel(gram_ref, home_ref, images_ref, modes_ref, new_images_ref, reduced_ref, table, turned_rows):
    packed = gram_ref[...]
    flipped = jnp.transpose(packed)
    down = lax.broadcasted_iota(jnp.int32, (WIDE, WIDE), 0)
    along = lax.broadcasted_iota(jnp.int32, (WIDE, WIDE), 1)
    diagonal = packed[:, NCOL : NCOL + 1]
    mass = jnp.where(down >= along, packed, flipped)
    stiff = jnp.where(down < along, packed, jnp.where(down == along, diagonal, flipped))
    mass = mass[:NCOL]
    stiff = stiff[:NCOL]
    column = along[:NCOL]
    level = lax.rsqrt(diagonal[:NCOL])
    level_row = lax.rsqrt(
        jnp.sum(jnp.where(down[:NCOL] == column, stiff, 0.0), axis=0, keepdims=True)
    )
    table[...] = level * jnp.where(column < NCOL, stiff * level_row, pltpu.roll(mass, NCOL, 1))
    block = 64
    row_in = lax.broadcasted_iota(jnp.int32, (8, 128), 0)
    full = (8, 128)
    for start in range(0, NCOL, block):
        used = range(start // 128, 2)
        panel = {
            (g, h): table[start + 8 * g : start + 8 * g + 8, 128 * h : 128 * h + 128]
            for g in range(block // 8)
            for h in used
        }
        for k in range(0, block, 2):
            side, lane = divmod(start + k, 128)
            group, place = divmod(k, 8)
            left = [jnp.broadcast_to(panel[g, side][:, lane : lane + 1], full) for g in range(block // 8)]
            right = [
                jnp.broadcast_to(panel[g, side][:, lane + 1 : lane + 2], full) for g in range(block // 8)
            ]
            a, b = left[group][place : place + 1], right[group][place : place + 1]
            c, d = left[group][place + 1 : place + 2], right[group][place + 1 : place + 2]
            inverse = 1.0 / (a * d - b * c)
            a, b, c, d = a * inverse, b * inverse, c * inverse, d * inverse
            for h in used:
                row, next_row = panel[group, h][place : place + 1], panel[group, h][place + 1 : place + 2]
                one = jnp.broadcast_to(d * row - b * next_row, full)
                two = jnp.broadcast_to(a * next_row - c * row, full)
                for g in range(block // 8):
                    swept = panel[g, h] - left[g] * one - right[g] * two
                    if g == group:
                        swept = jnp.where(
                            row_in == place, one, jnp.where(row_in == place + 1, two, swept)
                        )
                    panel[g, h] = swept
        whole = [jnp.concatenate([panel[g, h] for g in range(block // 8)], axis=0) for h in used]
        columns = table[:, start : start + block]
        for h in used:
            lanes = slice(128 * h, 128 * h + 128)
            table[:, lanes] = table[:, lanes] - dot(columns, whole[h - used[0]])
            table[start : start + block, lanes] = whole[h - used[0]]
    solved = jnp.where(
        lax.broadcasted_iota(jnp.int32, (NCOL, 128), 1) < MODES,
        level * pltpu.roll(table[:, 128:256], 64, 1),
        0.0,
    )
    weighed = dot(mass[:, :NCOL], solved)
    normal = dot(solved, weighed, ((0,), (0,)))[:MODES]
    row_in = lax.broadcasted_iota(jnp.int32, (MODES, 128), 0)
    lane = lax.broadcasted_iota(jnp.int32, (MODES, 128), 1)
    corner = jnp.where(lane == row_in, normal, 0.0)
    level = lax.rsqrt(jnp.sum(corner, axis=1, keepdims=True))
    level_row = lax.rsqrt(jnp.sum(corner, axis=0, keepdims=True))
    normal = jnp.where(
        lane < MODES,
        level * normal * level_row,
        jnp.where(lane == row_in + MODES, level, 0.0),
    )
    panel = [normal[8 * g : 8 * g + 8] for g in range(MODES // 8)]
    row_in = lax.broadcasted_iota(jnp.int32, (8, 128), 0)
    for k in range(0, MODES, 2):
        group, place = divmod(k, 8)
        rest = range(group, MODES // 8)
        left = {g: jnp.broadcast_to(panel[g][:, k : k + 1], full) for g in rest}
        right = {g: jnp.broadcast_to(panel[g][:, k + 1 : k + 2], full) for g in rest}
        a, b = left[group][place : place + 1], right[group][place : place + 1]
        c, d = left[group][place + 1 : place + 2], right[group][place + 1 : place + 2]
        first = lax.rsqrt(a)
        second = first * lax.rsqrt(a * d - b * c)
        row, next_row = panel[group][place : place + 1], panel[group][place + 1 : place + 2]
        one = row * first
        two = (a * next_row - c * row) * second
        one_over, two_over = one * first, two * second
        for g in rest:
            swept = panel[g] - left[g] * one_over - (a * right[g] - b * left[g]) * two_over
            if g == group:
                swept = jnp.where(row_in > place, swept, panel[g])
                swept = jnp.where(row_in == place, one, jnp.where(row_in == place + 1, two, swept))
            panel[g] = swept
    normal = jnp.concatenate(panel, axis=0)
    rotate = dot(solved[:, :MODES], normal[:, MODES:], ((1,), (1,)))
    turned = dot(stiff[:, :NCOL], rotate)
    reduced_ref[...] = dot(rotate, turned, ((0,), (0,)))
    rotate_parts = split(rotate)
    for source, target in ((home_ref, modes_ref), (images_ref, new_images_ref)):
        for c in range(3):
            turned_rows[:, :MODES] = split_dot(split(source[c][:, :NCOL]), rotate_parts)
            size_x = target.shape[1]
            size_y = turned_rows.shape[0] // size_x
            for y in range(0, size_y, 2):
                pair = [
                    turned_rows[pl.ds(y + odd, size_x, stride=size_y), :][:, :MODES]
                    for odd in range(2)
                ]
                target[c, :, y * MODES : (y + 2) * MODES] = jnp.concatenate(pair, axis=1)


def local(slabs, bands, basis, offsets, bond_modulus, bulk_modulus, springs, intact):
    size_x, size_y = offsets.shape[1:]
    home = size_x * size_y
    lattice, chosen, pick = constants(size_x, size_y)
    count = lattice.shape[1]
    devices = slabs * bands
    reduce_here = devices <= 32 and 32 % devices == 0
    total_rows = float(3 * home * devices)
    scalars = jnp.concatenate(
        [offsets, bond_modulus[None], bulk_modulus[None], springs[None]]
    )
    scalars = lax.optimization_barrier(scalars).reshape(6, home).T
    scalars = jnp.pad(scalars, ((0, 0), (0, WIDE - NCOL - 6)))[None]
    wide = jnp.concatenate(
        [basis.reshape(3, home, NCOL), jnp.pad(scalars, ((0, 2), (0, 0), (0, 0)))], axis=2
    )
    mask = jnp.sum(intact[0].astype(jnp.float32)[:, :, None] * chosen, axis=1)
    vmem = pl.BlockSpec(memory_space=pltpu.VMEM)
    f32 = jnp.float32
    images, gram = pl.pallas_call(
        functools.partial(
            plate_kernel, (size_x, size_y), slabs, bands, reduce_here, total_rows
        ),
        out_shape=(
            jax.ShapeDtypeStruct((3, home, WIDE), f32),
            jax.ShapeDtypeStruct((WIDE, WIDE), f32),
        ),
        in_specs=[vmem] * 4,
        out_specs=(vmem, vmem),
        scratch_shapes=[
            pltpu.VMEM((3, count, WIDE), f32),
            pltpu.VMEM((3, pick.shape[0], WIDE), f32),
            pltpu.VMEM((count, WIDE), f32),
            pltpu.VMEM((pick.shape[0], WIDE), f32),
            pltpu.VMEM((3 * home, 3 * count), jnp.bfloat16),
            pltpu.VMEM((3 * home, 3 * count), jnp.bfloat16),
            pltpu.VMEM((3 * home, count), jnp.bfloat16),
            pltpu.VMEM((3 * home, count), jnp.bfloat16),
            pltpu.VMEM((home, 3 * count), jnp.bfloat16),
            pltpu.VMEM((home, 3 * count), jnp.bfloat16),
            pltpu.VMEM((3 * count, WIDE), jnp.bfloat16),
            pltpu.VMEM((3 * count, WIDE), jnp.bfloat16),
            pltpu.VMEM((WIDE, WIDE), f32),
            pltpu.VMEM((devices, max(WIDE // devices, 8), WIDE), f32),
            pltpu.VMEM((max(WIDE // devices, 8), WIDE), f32),
        ]
        + [pltpu.SemaphoreType.DMA((24,))] * 4
        + [pltpu.SemaphoreType.DMA((devices,))] * 4,
        compiler_params=pltpu.CompilerParams(
            collective_id=0, has_side_effects=True, vmem_limit_bytes=48 << 20
        ),
    )(wide, mask, lattice, pick)
    if not reduce_here:
        gram = lax.psum(gram, ("slab", "band"))
    modes, new_images, reduced = pl.pallas_call(
        mode_kernel,
        out_shape=(
            jax.ShapeDtypeStruct((3, size_x, size_y * MODES), f32),
            jax.ShapeDtypeStruct((3, size_x, size_y * MODES), f32),
            jax.ShapeDtypeStruct((MODES, MODES), f32),
        ),
        in_specs=[vmem] * 3,
        out_specs=(vmem,) * 3,
        scratch_shapes=[pltpu.VMEM((NCOL, WIDE), f32), pltpu.VMEM((home, 128), f32)],
        compiler_params=pltpu.CompilerParams(vmem_limit_bytes=48 << 20),
    )(gram, wide, images)
    return modes, new_images, reduced


def solution(mesh):
    in_specs = (
        P(None, "slab", "band"),
        P(None, "slab", "band"),
        P("slab", "band"),
        P("slab", "band"),
        P("slab", "band"),
        P("slab", "band", None),
    )
    out_specs = (P(None, "slab", "band"), P(None, "slab", "band"), P())
    body = functools.partial(local, mesh.shape["slab"], mesh.shape["band"])
    return jax.shard_map(body, mesh=mesh, in_specs=in_specs, out_specs=out_specs, check_vma=False)
```

```python
import functools

import jax
import jax.numpy as jnp
import numpy as np
from jax import lax
from jax.experimental import pallas as pl
from jax.experimental.pallas import tpu as pltpu
from jax.sharding import PartitionSpec as P

BLOCK_X = 16
BLOCK_Y = 8
REACH = 3
MODES = 64
NCOL = 192
WIDE = 256
MESH = pl.DeviceIdType.MESH
horizon_square = 9.0
bond_scale = 1.0 / 18.0
dilation_scale = 1.0 / 27.0


def dot(a, b, contract=((1,), (0,))):
    return lax.dot_general(
        a,
        b,
        (contract, ((), ())),
        precision=lax.Precision.HIGHEST,
        preferred_element_type=jnp.float32,
    )


def split(value):
    high = value.astype(jnp.bfloat16)
    return high, (value - high.astype(jnp.float32)).astype(jnp.bfloat16)


def narrow_dot(a, b, contract=((1,), (0,))):
    return lax.dot_general(
        a, b, (contract, ((), ())), preferred_element_type=jnp.float32
    )


def split_dot(a, b, contract=((1,), (0,))):
    small = narrow_dot(a[0], b[1], contract) + narrow_dot(a[1], b[0], contract)
    return small + narrow_dot(a[0], b[0], contract)


def picked(pick, value):
    first, rest = split(value)
    second = value - first.astype(jnp.float32)
    third = (second - rest.astype(jnp.float32)).astype(jnp.bfloat16)
    return narrow_dot(pick, first) + (narrow_dot(pick, rest) + narrow_dot(pick, third))


def far_lattice(size_x, size_y):
    points = [(x, y) for x in range(size_x) for y in range(size_y)]
    low, high_x, high_y = range(-REACH, 0), range(size_x, size_x + REACH), range(size_y, size_y + REACH)
    points += [(x, y) for x in low for y in range(size_y)]
    points += [(x, y) for x in high_x for y in range(size_y)]
    points += [(x, y) for x in range(size_x) for y in low]
    points += [(x, y) for x in range(size_x) for y in high_y]
    for side_x in (low, high_x):
        for side_y in (low, high_y):
            points += [(x, y) for x in side_x for y in side_y] + [None] * (16 - REACH * REACH)
    return points


def constants(size_x, size_y):
    points = far_lattice(size_x, size_y)
    count = len(points)
    blocks = size_y // BLOCK_Y
    lattice = np.zeros((8, count), np.float32)
    chosen = np.zeros((blocks, 9, count), np.float32)
    for k, point in enumerate(points):
        if point is None:
            continue
        lattice[0, k], lattice[1, k] = point
        for b in range(blocks):
            dx, dy = point[0] // BLOCK_X, point[1] // BLOCK_Y - b
            if abs(dx) <= 1 and abs(dy) <= 1:
                chosen[b, 3 * (dx + 1) + dy + 1, k] = 1.0
    rows = [(x, y) for x in range(size_x) for y in range(REACH)]
    rows += [(x, y) for x in range(size_x) for y in range(size_y - REACH, size_y)]
    for side_x in (range(REACH), range(size_x - REACH, size_x)):
        for side_y in (range(REACH), range(size_y - REACH, size_y)):
            rows += [(x, y) for x in side_x for y in side_y] + [None] * (16 - REACH * REACH)
    pick = np.zeros((len(rows), size_x * size_y), np.float32)
    for r, point in enumerate(rows):
        if point is not None:
            pick[r, point[0] * size_y + point[1]] = 1.0
    return lattice, chosen, pick.astype(jnp.bfloat16)


def plate_kernel(
    shape,
    slabs,
    bands,
    reduce_here,
    total_rows,
    home_ref,
    mask_ref,
    lattice_ref,
    pick_ref,
    images_ref,
    gram_ref,
    far,
    edge,
    theta,
    theta_edge,
    tensor,
    tensor_low,
    lean,
    lean_low,
    volume_lean,
    volume_lean_low,
    field,
    field_low,
    part,
    slots,
    mine,
    halo_send,
    halo_recv,
    theta_send,
    theta_recv,
    scatter_send,
    scatter_recv,
    gather_send,
    gather_recv,
):
    size_x, size_y = shape
    home = size_x * size_y
    edge_x, edge_y = REACH * size_y, REACH * size_x
    slab, band = lax.axis_index("slab"), lax.axis_index("band")
    devices = slabs * bands
    me = slab * bands + band
    left, right = lax.rem(slab + slabs - 1, slabs), lax.rem(slab + 1, slabs)
    down, up = lax.rem(band + bands - 1, bands), lax.rem(band + 1, bands)

    def peer(step):
        other = lax.rem(me + step, devices)
        return other, (lax.div(other, bands), lax.rem(other, bands))

    around = [
        (left, band), (right, band), (slab, down), (slab, up),
        (left, down), (left, up), (right, down), (right, up),
    ]
    barrier = pltpu.get_barrier_semaphore()
    if reduce_here:
        for step in range(1, devices):
            pl.semaphore_signal(barrier, inc=1, device_id=peer(step)[1], device_id_type=MESH)
    else:
        for target in around:
            pl.semaphore_signal(barrier, inc=1, device_id=target, device_id_type=MESH)

    at = [home, home + edge_x, home + 2 * edge_x, home + 2 * edge_x + edge_y]
    corner = home + 2 * edge_x + 2 * edge_y
    has_left, has_right = slab > 0, slab < slabs - 1
    has_down, has_up = band > 0, band < bands - 1
    exists = [
        has_left, has_right, has_down, has_up,
        has_left & has_down, has_left & has_up, has_right & has_down, has_right & has_up,
    ]
    opposite = [1, 0, 3, 2, 7, 6, 5, 4]
    plan = [
        (True, 0, edge_x, at[1], around[0]),
        (True, home - edge_x, edge_x, at[0], around[1]),
        (False, 0, edge_y, at[3], around[2]),
        (False, edge_y, edge_y, at[2], around[3]),
        (False, 2 * edge_y, 16, corner + 48, around[4]),
        (False, 2 * edge_y + 16, 16, corner + 32, around[5]),
        (False, 2 * edge_y + 32, 16, corner + 16, around[6]),
        (False, 2 * edge_y + 48, 16, corner, around[7]),
    ]
    for c in range(3):
        edge[c] = picked(pick_ref[...], home_ref[c])
    pl.semaphore_wait(barrier, devices - 1 if reduce_here else 8)
    pieces = [
        (pl.ds(0, 1), pl.ds(128, 128)),
        (pl.ds(0, 1), pl.ds(0, 128)),
        (pl.ds(1, 2), pl.ds(0, WIDE)),
    ]
    halo = []
    for number, (direct, start, rows, there, target) in enumerate(plan):
        source = home_ref if direct else edge
        copies = []
        for piece, (parts, lanes) in enumerate(pieces):
            copy = pltpu.make_async_remote_copy(
                src_ref=source.at[parts, pl.ds(start, rows), lanes],
                dst_ref=far.at[parts, pl.ds(there, rows), lanes],
                send_sem=halo_send.at[3 * number + piece],
                recv_sem=halo_recv.at[3 * number + piece],
                device_id=target,
                device_id_type=MESH,
            )
            copies.append(copy)
        pl.when(exists[number])(copies[0].start)
        halo.append(copies)

        @pl.when(jnp.logical_not(exists[opposite[number]]))
        def clear(there=there, rows=rows):
            far[:, pl.ds(there, rows), :] = jnp.zeros((3, rows, WIDE), jnp.float32)
            theta[pl.ds(there, rows), :] = jnp.zeros((rows, WIDE), jnp.float32)
    for number, copies in enumerate(halo):
        for copy in copies[1:]:
            pl.when(exists[number])(copy.start)
    far[:, pl.ds(0, home), :] = home_ref[...]
    home_parts = split(home_ref[...].reshape(3 * home, WIDE))
    mass = split_dot(home_parts, home_parts, ((0,), (0,)))
    for number, copies in enumerate(halo):
        pl.when(exists[opposite[number]])(copies[0].wait_recv)

    rows_far = jnp.transpose(far[0, :, 128:256])
    count = rows_far.shape[1]
    chunk = 64
    blocks = size_y // BLOCK_Y
    masks = jnp.broadcast_to(
        mask_ref[...].reshape(1, blocks, 1, count), (chunk // size_y, blocks, BLOCK_Y, count)
    ).reshape(chunk, count)
    lattice_x, lattice_y = lattice_ref[0:1, :], lattice_ref[1:2, :]

    @pl.loop(0, home // chunk)
    def build(number):
        first = pl.multiple_of(number * chunk, chunk)
        side = home_ref[0, pl.ds(first, chunk), 128:256]
        point = lax.broadcasted_iota(jnp.int32, (chunk, 1), 0) + first
        home_x = (point // size_y).astype(jnp.float32)
        home_y = (point % size_y).astype(jnp.float32)
        bond = [
            (lattice_x - home_x) + (rows_far[64:65, :] - side[:, 64:65]),
            (lattice_y - home_y) + (rows_far[65:66, :] - side[:, 65:66]),
            rows_far[66:67, :] - side[:, 66:67],
        ]
        distance = bond[0] * bond[0] + bond[1] * bond[1] + bond[2] * bond[2]
        weight = jnp.maximum(1.0 - distance / horizon_square, 0.0) * masks
        coupling = weight * ((side[:, 67:68] + rows_far[67:68, :]) * bond_scale)
        itself = lax.broadcasted_iota(jnp.int32, (chunk, count), 1) == point
        springs = side[:, 69:70]
        for c in range(3):
            weighted = weight * bond[c]
            added = jnp.where(itself, jnp.sum(weighted, axis=1, keepdims=True), 0.0)
            rows = pl.ds(c * home + first, chunk)
            lean[rows, :], lean_low[rows, :] = split(weighted + added)
            here = (pl.ds(first, chunk), slice(c * count, (c + 1) * count))
            volume_lean[here], volume_lean_low[here] = split(weighted - added)
            leading = coupling * bond[c]
            for d in range(c, 3):
                entry = leading * bond[d]
                own = jnp.sum(entry, axis=1, keepdims=True)
                if c == d:
                    own = own + springs
                high, low = split(jnp.where(itself, own, 0.0) - entry)
                here = (rows, slice(d * count, (d + 1) * count))
                tensor[here], tensor_low[here] = high, low
                if c != d:
                    here = (pl.ds(d * home + first, chunk), slice(c * count, (c + 1) * count))
                    tensor[here], tensor_low[here] = high, low

    for number, copies in enumerate(halo):
        for copy in copies[1:]:
            pl.when(exists[opposite[number]])(copy.wait_recv)
    field[...], field_low[...] = split(far[...].reshape(3 * count, WIDE))
    field_parts = (field[...], field_low[...])
    volume = split_dot((volume_lean[...], volume_lean_low[...]), field_parts)
    theta[pl.ds(0, home), :] = volume * (home_ref[0, :, 196:197] * dilation_scale)
    theta_edge[...] = picked(pick_ref[...], theta[pl.ds(0, home), :])
    moved = []
    for number, (direct, start, rows, there, target) in enumerate(plan):
        source = theta if direct else theta_edge
        copy = pltpu.make_async_remote_copy(
            src_ref=source.at[pl.ds(start, rows), :],
            dst_ref=theta.at[pl.ds(there, rows), :],
            send_sem=theta_send.at[number],
            recv_sem=theta_recv.at[number],
            device_id=target,
            device_id_type=MESH,
        )
        pl.when(exists[number])(copy.start)
        moved.append(copy)

    @pl.loop(0, 3)
    def forces(c):
        rows = pl.ds(pl.multiple_of(c * home, home), home)
        images_ref[c] = split_dot((tensor[rows, :], tensor_low[rows, :]), (field[...], field_low[...]))

    for number, copy in enumerate(moved):
        pl.when(exists[opposite[number]])(copy.wait_recv)
    theta_parts = split(theta[...])
    images = images_ref[...].reshape(3 * home, WIDE) - split_dot(
        (lean[...], lean_low[...]), theta_parts
    )
    images_ref[...] = images.reshape(3, home, WIDE)
    stiff = split_dot(home_parts, split(images), ((0,), (0,)))
    stiff = 0.5 * (stiff + jnp.transpose(stiff))
    down_axis = lax.broadcasted_iota(jnp.int32, (WIDE, WIDE), 0)
    along = lax.broadcasted_iota(jnp.int32, (WIDE, WIDE), 1)
    own = jnp.sum(jnp.where(down_axis == along, stiff, 0.0), axis=1, keepdims=True)
    packed = jnp.where(along == NCOL, own, jnp.where(down_axis >= along, mass, stiff))
    packed = packed * (1.0 / total_rows)
    if not reduce_here:
        gram_ref[...] = packed
    else:
        part[...] = packed
        share = WIDE // devices
        copies = []
        for step in range(1, devices):
            other, target = peer(step)
            copy = pltpu.make_async_remote_copy(
                src_ref=part.at[pl.ds(pl.multiple_of(other * share, share), share), :],
                dst_ref=slots.at[step],
                send_sem=scatter_send.at[step],
                recv_sem=scatter_recv.at[step],
                device_id=target,
                device_id_type=MESH,
            )
            pl.when(other * share < NCOL)(copy.start)
            copies.append(copy)
        here = pl.ds(pl.multiple_of(me * share, share), share)
        owner = me * share < NCOL
        gram_ref[NCOL:, :] = jnp.zeros((WIDE - NCOL, WIDE), jnp.float32)

        @pl.when(owner)
        def add_up():
            total = part[here, :]
            for step in range(1, devices):
                copies[step - 1].wait_recv()
                total = total + slots[step]
            mine[...] = total
            gram_ref[here, :] = total

        gathers = []
        for step in range(1, devices):
            copy = pltpu.make_async_remote_copy(
                src_ref=mine,
                dst_ref=gram_ref.at[here, :],
                send_sem=gather_send.at[step],
                recv_sem=gather_recv.at[step],
                device_id=peer(step)[1],
                device_id_type=MESH,
            )
            pl.when(owner)(copy.start)
            gathers.append(copy)
        for step in range(1, devices):
            pl.when(peer(devices - step)[0] * share < NCOL)(gathers[step - 1].wait_recv)
        for step in range(1, devices):
            pl.when(peer(step)[0] * share < NCOL)(copies[step - 1].wait_send)
            pl.when(owner)(gathers[step - 1].wait_send)
    for number in range(8):
        for copy in halo[number]:
            pl.when(exists[number])(copy.wait_send)
        pl.when(exists[number])(moved[number].wait_send)


def mode_kernel(gram_ref, home_ref, images_ref, modes_ref, new_images_ref, reduced_ref, table, turned_rows):
    packed = gram_ref[...]
    flipped = jnp.transpose(packed)
    down = lax.broadcasted_iota(jnp.int32, (WIDE, WIDE), 0)
    along = lax.broadcasted_iota(jnp.int32, (WIDE, WIDE), 1)
    diagonal = packed[:, NCOL : NCOL + 1]
    mass = jnp.where(down >= along, packed, flipped)
    stiff = jnp.where(down < along, packed, jnp.where(down == along, diagonal, flipped))
    mass = mass[:NCOL]
    stiff = stiff[:NCOL]
    column = along[:NCOL]
    level = lax.rsqrt(diagonal[:NCOL])
    level_row = lax.rsqrt(
        jnp.sum(jnp.where(down[:NCOL] == column, stiff, 0.0), axis=0, keepdims=True)
    )
    table[...] = level * jnp.where(column < NCOL, stiff * level_row, pltpu.roll(mass, NCOL, 1))
    block = 64
    row_in = lax.broadcasted_iota(jnp.int32, (8, 128), 0)
    full = (8, 128)
    for start in range(0, NCOL, block):
        used = range(start // 128, 2)
        panel = {
            (g, h): table[start + 8 * g : start + 8 * g + 8, 128 * h : 128 * h + 128]
            for g in range(block // 8)
            for h in used
        }
        for k in range(0, block, 2):
            side, lane = divmod(start + k, 128)
            group, place = divmod(k, 8)
            left = [jnp.broadcast_to(panel[g, side][:, lane : lane + 1], full) for g in range(block // 8)]
            right = [
                jnp.broadcast_to(panel[g, side][:, lane + 1 : lane + 2], full) for g in range(block // 8)
            ]
            a, b = left[group][place : place + 1], right[group][place : place + 1]
            c, d = left[group][place + 1 : place + 2], right[group][place + 1 : place + 2]
            inverse = 1.0 / (a * d - b * c)
            a, b, c, d = a * inverse, b * inverse, c * inverse, d * inverse
            for h in used:
                row, next_row = panel[group, h][place : place + 1], panel[group, h][place + 1 : place + 2]
                one = jnp.broadcast_to(d * row - b * next_row, full)
                two = jnp.broadcast_to(a * next_row - c * row, full)
                for g in range(block // 8):
                    swept = panel[g, h] - left[g] * one - right[g] * two
                    if g == group:
                        swept = jnp.where(
                            row_in == place, one, jnp.where(row_in == place + 1, two, swept)
                        )
                    panel[g, h] = swept
        whole = [jnp.concatenate([panel[g, h] for g in range(block // 8)], axis=0) for h in used]
        columns = table[:, start : start + block]
        for h in used:
            lanes = slice(128 * h, 128 * h + 128)
            table[:, lanes] = table[:, lanes] - dot(columns, whole[h - used[0]])
            table[start : start + block, lanes] = whole[h - used[0]]
    solved = jnp.where(
        lax.broadcasted_iota(jnp.int32, (NCOL, 128), 1) < MODES,
        level * pltpu.roll(table[:, 128:256], 64, 1),
        0.0,
    )
    weighed = dot(mass[:, :NCOL], solved)
    normal = dot(solved, weighed, ((0,), (0,)))[:MODES]
    row_in = lax.broadcasted_iota(jnp.int32, (MODES, 128), 0)
    lane = lax.broadcasted_iota(jnp.int32, (MODES, 128), 1)
    corner = jnp.where(lane == row_in, normal, 0.0)
    level = lax.rsqrt(jnp.sum(corner, axis=1, keepdims=True))
    level_row = lax.rsqrt(jnp.sum(corner, axis=0, keepdims=True))
    normal = jnp.where(
        lane < MODES,
        level * normal * level_row,
        jnp.where(lane == row_in + MODES, level, 0.0),
    )
    panel = [normal[8 * g : 8 * g + 8] for g in range(MODES // 8)]
    row_in = lax.broadcasted_iota(jnp.int32, (8, 128), 0)
    for k in range(0, MODES, 2):
        group, place = divmod(k, 8)
        rest = range(group, MODES // 8)
        left = {g: jnp.broadcast_to(panel[g][:, k : k + 1], full) for g in rest}
        right = {g: jnp.broadcast_to(panel[g][:, k + 1 : k + 2], full) for g in rest}
        a, b = left[group][place : place + 1], right[group][place : place + 1]
        c, d = left[group][place + 1 : place + 2], right[group][place + 1 : place + 2]
        first = lax.rsqrt(a)
        second = first * lax.rsqrt(a * d - b * c)
        row, next_row = panel[group][place : place + 1], panel[group][place + 1 : place + 2]
        one = row * first
        two = (a * next_row - c * row) * second
        one_over, two_over = one * first, two * second
        for g in rest:
            swept = panel[g] - left[g] * one_over - (a * right[g] - b * left[g]) * two_over
            if g == group:
                swept = jnp.where(row_in > place, swept, panel[g])
                swept = jnp.where(row_in == place, one, jnp.where(row_in == place + 1, two, swept))
            panel[g] = swept
    normal = jnp.concatenate(panel, axis=0)
    rotate = dot(solved[:, :MODES], normal[:, MODES:], ((1,), (1,)))
    turned = dot(stiff[:, :NCOL], rotate)
    reduced_ref[...] = dot(rotate, turned, ((0,), (0,)))
    rotate_parts = split(rotate)
    for source, target in ((home_ref, modes_ref), (images_ref, new_images_ref)):
        for c in range(3):
            turned_rows[:, :MODES] = split_dot(split(source[c][:, :NCOL]), rotate_parts)
            size_x = target.shape[1]
            size_y = turned_rows.shape[0] // size_x
            for y in range(0, size_y, 2):
                pair = [
                    turned_rows[pl.ds(y + odd, size_x, stride=size_y), :][:, :MODES]
                    for odd in range(2)
                ]
                target[c, :, y * MODES : (y + 2) * MODES] = jnp.concatenate(pair, axis=1)


def local(slabs, bands, basis, offsets, bond_modulus, bulk_modulus, springs, intact):
    size_x, size_y = offsets.shape[1:]
    home = size_x * size_y
    lattice, chosen, pick = constants(size_x, size_y)
    count = lattice.shape[1]
    devices = slabs * bands
    reduce_here = devices <= 32 and 32 % devices == 0
    total_rows = float(3 * home * devices)
    scalars = jnp.concatenate(
        [offsets, bond_modulus[None], bulk_modulus[None], springs[None]]
    )
    scalars = lax.optimization_barrier(scalars).reshape(6, home).T
    scalars = jnp.pad(scalars, ((0, 0), (0, WIDE - NCOL - 6)))[None]
    wide = jnp.concatenate(
        [basis.reshape(3, home, NCOL), jnp.pad(scalars, ((0, 2), (0, 0), (0, 0)))], axis=2
    )
    mask = jnp.sum(intact[0].astype(jnp.float32)[:, :, None] * chosen, axis=1)
    vmem = pl.BlockSpec(memory_space=pltpu.VMEM)
    f32 = jnp.float32
    images, gram = pl.pallas_call(
        functools.partial(
            plate_kernel, (size_x, size_y), slabs, bands, reduce_here, total_rows
        ),
        out_shape=(
            jax.ShapeDtypeStruct((3, home, WIDE), f32),
            jax.ShapeDtypeStruct((WIDE, WIDE), f32),
        ),
        in_specs=[vmem] * 4,
        out_specs=(vmem, vmem),
        scratch_shapes=[
            pltpu.VMEM((3, count, WIDE), f32),
            pltpu.VMEM((3, pick.shape[0], WIDE), f32),
            pltpu.VMEM((count, WIDE), f32),
            pltpu.VMEM((pick.shape[0], WIDE), f32),
            pltpu.VMEM((3 * home, 3 * count), jnp.bfloat16),
            pltpu.VMEM((3 * home, 3 * count), jnp.bfloat16),
            pltpu.VMEM((3 * home, count), jnp.bfloat16),
            pltpu.VMEM((3 * home, count), jnp.bfloat16),
            pltpu.VMEM((home, 3 * count), jnp.bfloat16),
            pltpu.VMEM((home, 3 * count), jnp.bfloat16),
            pltpu.VMEM((3 * count, WIDE), jnp.bfloat16),
            pltpu.VMEM((3 * count, WIDE), jnp.bfloat16),
            pltpu.VMEM((WIDE, WIDE), f32),
            pltpu.VMEM((devices, max(WIDE // devices, 8), WIDE), f32),
            pltpu.VMEM((max(WIDE // devices, 8), WIDE), f32),
        ]
        + [pltpu.SemaphoreType.DMA((24,))] * 4
        + [pltpu.SemaphoreType.DMA((devices,))] * 4,
        compiler_params=pltpu.CompilerParams(
            collective_id=0, has_side_effects=True, vmem_limit_bytes=48 << 20
        ),
    )(wide, mask, lattice, pick)
    if not reduce_here:
        gram = lax.psum(gram, ("slab", "band"))
    modes, new_images, reduced = pl.pallas_call(
        mode_kernel,
        out_shape=(
            jax.ShapeDtypeStruct((3, size_x, size_y * MODES), f32),
            jax.ShapeDtypeStruct((3, size_x, size_y * MODES), f32),
            jax.ShapeDtypeStruct((MODES, MODES), f32),
        ),
        in_specs=[vmem] * 3,
        out_specs=(vmem,) * 3,
        scratch_shapes=[pltpu.VMEM((NCOL, WIDE), f32), pltpu.VMEM((home, 128), f32)],
        compiler_params=pltpu.CompilerParams(vmem_limit_bytes=48 << 20),
    )(gram, wide, images)
    return modes, new_images, reduced


def solution(mesh):
    in_specs = (
        P(None, "slab", "band"),
        P(None, "slab", "band"),
        P("slab", "band"),
        P("slab", "band"),
        P("slab", "band"),
        P("slab", "band", None),
    )
    out_specs = (P(None, "slab", "band"), P(None, "slab", "band"), P())
    body = functools.partial(local, mesh.shape["slab"], mesh.shape["band"])
    return jax.shard_map(body, mesh=mesh, in_specs=in_specs, out_specs=out_specs, check_vma=False)
```
